32 devices in a mesh: row: 16 (over z, y, x), col: 2 (over core).
Axes of the slice: x: 2, y: 2, z: 4, core: 2. Of those that a mesh axis runs over, the one named last changes fastest.
Arguments:
- features: bfloat16 [128, 4096], P('col', 'row'), may hold values from -6 to 6
- order: int32 [4096], P('row'), may hold values from 0 to 4095, as said below
- weight: bfloat16 [128, 256], P(None, 'col'), may hold values from -0.5 to 0.5
- bias: bfloat16 [256], P('col'), may hold values from -3 to 3
- tiles: bfloat16 [32, 64, 128, 128], P('row'), may hold values from -0.09375 to 0.09375
- coords: int32 [32, 64], P('row'), may hold values from 0 to 31
- counts: int32 [32], P('row'), may hold values from 1 to 64, 1024 in all
- grad_hidden: bfloat16 [256, 4096], P('col', 'row'), may hold values from -6 to 6
Outputs:
- hidden: bfloat16 [256, 4096], P('col', 'row')
- grad_features: float32 [128, 4096], P('col', 'row')
- grad_weight: float32 [128, 256], P(None, 'col')
- grad_bias: float32 [256], P('col')
The draws below stay inside these ranges and needn't reach their ends.
Inputs may be any that keep to these rules, and one draw needn't show every extreme that they name: Within each aligned block of 256 nodes, order is a permutation of that block's node indices. `counts`: some block row fills all 64 slots. `coords`: slots of one block row may name the same column block.
All inputs are finite; a program needn't handle non-finite values.
Results may differ from the reference program's by a relative error of at most 0.0015.
Values may be sent and summed in bfloat16 or wider, within the bound.
A program may use at most 64 MiB of HBM per device.

```python
import math
import jax
import jax.numpy as jnp
import numpy as np
from jax import lax

FIN = 128
HID = 256
TILE = 128
K = 64
BR_DEV = 2
BLOCKS = 32
ROWS_DEV = 256
NODES = 4096


def draw_order(key, part):
    groups = BLOCKS // BR_DEV
    sub_keys = jax.random.split(key, groups)
    shuffled = jax.vmap(lambda one_key: jax.random.permutation(one_key, ROWS_DEV))(sub_keys)
    offsets = jnp.arange(groups, dtype=jnp.int32)[:, None] * ROWS_DEV
    return (shuffled.astype(jnp.int32) + offsets).reshape(-1)


def touch_ends(array, key, low, top_value):
    place = [jax.random.randint(jax.random.fold_in(key, axis), (), 0, length) for axis, length in enumerate(array.shape)]
    main_axis = array.shape.index(max(array.shape))
    beside = place[:main_axis] + [(place[main_axis] + 1) % array.shape[main_axis]] + place[main_axis + 1:]
    return array.at[tuple(place)].set(low).at[tuple(beside)].set(top_value)


def level_of(own_key, extent, cuts, low, top_value):
    loudness, own = 1.0, jax.random.fold_in(own_key, 6)
    for axis_at, shards_of in cuts:
        heights = jnp.exp(jax.random.uniform(jax.random.fold_in(own, axis_at), (shards_of,), jnp.float32, low / len(cuts), top_value / len(cuts)))
        loudness = loudness * jnp.repeat(heights, extent[axis_at] // shards_of).reshape([-1 if axis == axis_at else 1 for axis in range(len(extent))])
    return loudness


def split_up(count, total, most, lean):
    weights = [(1 << 20) // math.isqrt(rank ** lean) + 1 for rank in range(2, count + 1)]
    surplus, given = total - most - (count - 1), [1] * (count - 1)
    while surplus > 0:
        free = [i for i in range(count - 1) if given[i] < most]
        mass, budget = sum([weights[i] for i in free]), surplus
        for i in free:
            more = min(most - given[i], max(1, budget * weights[i] // mass), surplus)
            given[i] = given[i] + more
            surplus = surplus - more
    return np.array([most] + given)


def ragged(rng, amount, total, most, slope):
    if amount == 2:
        one = jax.random.randint(rng, (), max(1, total - most), min(most, total - 1) + 1)
        return jnp.stack([one, total - one])
    lengths = jnp.asarray(split_up(amount, total, most, slope), jnp.int32)
    couples = (amount - 1) // 2
    source_of, receiver = lengths[1:1 + 2 * couples:2], lengths[2:2 + 2 * couples:2]
    slack = jnp.minimum(source_of - 1, most - receiver)
    moved = jax.random.randint(jax.random.fold_in(rng, 1), (couples,), 0, 1 << 20) % (slack + 1)
    lengths = lengths.at[1:1 + 2 * couples:2].set(source_of - moved).at[2:2 + 2 * couples:2].set(receiver + moved)
    return lengths[jax.random.permutation(jax.random.fold_in(rng, 2), amount)]


def gaussian(stream_key, extent, deviation, reach, shards=(), kind=jnp.bfloat16):
    values = jax.random.normal(stream_key, extent, jnp.float32) * deviation
    if len(shards) > 0:
        values = level_of(stream_key, extent, shards, -0.22, 0.18) * values
    return jnp.clip(values, min=-reach, max=reach).astype(kind)


def setup_inputs(seed: int = 0) -> dict:
    streams_of = jax.random.split(jax.random.key(seed), 9)
    features = gaussian(streams_of[0], (FIN, NODES), 1.0, 6.0, ((0, 2), (1, 16)))
    order = draw_order(jax.random.fold_in(streams_of[8], 71), 0)
    weight = gaussian(streams_of[2], (FIN, HID), FIN ** -0.5, 0.5, ((1, 2),))
    bias = gaussian(streams_of[3], (HID,), 0.5, 3.0, ((0, 2),))
    tiles = gaussian(streams_of[4], (BLOCKS, K, TILE, TILE), (K * TILE // 2) ** -0.5, 0.09375, ((0, 16),))
    coords = touch_ends(jax.random.randint(streams_of[5], (BLOCKS, K), 0, BLOCKS), jax.random.fold_in(streams_of[5], 1), 0, BLOCKS - 1).astype(jnp.int32)
    counts = ragged(streams_of[6], BLOCKS, BLOCKS * K // 2, K, 2).astype(jnp.int32)
    grad_hidden = gaussian(streams_of[7], (HID, NODES), 1.0, 6.0, ((0, 2), (1, 16)))
    return {"features": features, "order": order, "weight": weight, "bias": bias, "tiles": tiles, "coords": coords, "counts": counts, "grad_hidden": grad_hidden}


def reference(features, order, weight, bias, tiles, coords, counts, grad_hidden):
    reordered = features[:, order]
    slot_live = (jnp.arange(K, dtype=jnp.int32)[None, :] < counts[:, None]).astype(jnp.float32)
    projected = jnp.dot(weight.T, reordered, preferred_element_type=jnp.float32)
    projected_blocks = projected.reshape(HID, BLOCKS, TILE)

    def forward_row(inputs):
        tile_row, coord_row, live_row = inputs
        picked = projected_blocks[:, coord_row, :] * live_row[None, :, None]
        return jnp.einsum('fkc,krc->fr', picked, tile_row.astype(jnp.float32), precision=lax.Precision.HIGHEST)
    summed = lax.map(forward_row, (tiles, coords, slot_live))
    pre_act = jnp.transpose(summed, (1, 0, 2)).reshape(HID, NODES) + bias.astype(jnp.float32)[:, None]
    gate_value = jax.nn.sigmoid(pre_act)
    hidden = (pre_act * gate_value).astype(jnp.bfloat16)
    grad_pre = grad_hidden.astype(jnp.float32) * gate_value * (1.0 + pre_act * (1.0 - gate_value))
    grad_blocks = jnp.transpose(grad_pre.reshape(HID, BLOCKS, TILE), (1, 0, 2))

    def backward_row(carry, inputs):
        tile_row, coord_row, live_row, grad_row = inputs
        contrib = jnp.einsum('fr,krc->kfc', grad_row, tile_row.astype(jnp.float32), precision=lax.Precision.HIGHEST)
        contrib = contrib * live_row[:, None, None]
        carry = carry.at[:, coord_row, :].add(jnp.transpose(contrib, (1, 0, 2)))
        return (carry, None)
    start_sum = jnp.zeros((HID, BLOCKS, TILE), jnp.float32)
    column_grad, _ = lax.scan(backward_row, start_sum, (tiles, coords, slot_live, grad_blocks))
    column_grad = column_grad.reshape(HID, NODES)
    grad_features = jnp.dot(weight.astype(jnp.float32), column_grad, precision=lax.Precision.HIGHEST)
    norm_factor = 1.0 / math.sqrt(NODES)
    grad_weight = jnp.dot(reordered.astype(jnp.float32), column_grad.T, precision=lax.Precision.HIGHEST) * norm_factor
    grad_bias = lax.optimization_barrier(jnp.sum(grad_pre, axis=1)) * norm_factor
    return (hidden, grad_features, grad_weight, grad_bias)
```

```python
import functools
import math

import jax
import jax.numpy as jnp
from jax import lax
from jax.experimental import pallas as pl
from jax.experimental.pallas import tpu as pltpu
from jax.sharding import PartitionSpec as P

MESH = pl.DeviceIdType.MESH
F32 = jnp.float32
BF16 = jnp.bfloat16
GROUP = 8
VMEM_LIMIT = 56 * 1024 * 1024

NN = (((1,), (0,)), ((), ()))
NT = (((1,), (1,)), ((), ()))
TN = (((0,), (0,)), ((), ()))


def mm(a, b, dims):
    return lax.dot_general(a, b, dims, preferred_element_type=F32)


def split(x):
    hi = x.astype(BF16)
    return hi, (x - hi.astype(F32)).astype(BF16)


def build_kernel(tiles, coords, counts, hi_ref, lo_ref, buf, acc, sems):
    rows, slots, tile, _ = buf.shape
    groups = slots // GROUP

    def copy(i, g):
        part = pl.ds(g * GROUP, GROUP)
        return pltpu.make_async_copy(tiles.at[i, part], buf.at[i, part], sems.at[i, g])

    for g in range(groups):
        for i in range(rows):
            @pl.when(counts[i] > g * GROUP)
            def _():
                copy(i, g).start()
    acc[...] = jnp.zeros_like(acc)
    for g in range(groups):
        for i in range(rows):
            live = jnp.clip(counts[i] - g * GROUP, 0, GROUP)

            @pl.when(live > 0)
            def _():
                copy(i, g).wait()

                def add(k, carry):
                    at = g * GROUP + k
                    j = coords[i, at]
                    mine = pl.ds(i * tile, tile)
                    acc[j, mine, :] = acc[j, mine, :] + buf[i, at].astype(F32)
                    return carry

                lax.fori_loop(0, live, add, 0)
    pieces = hi_ref.shape[0]

    def convert(p, carry):
        for h in range(rows):
            hi, lo = split(acc[p * rows + h])
            hi_ref[p, :, h * tile:(h + 1) * tile] = hi
            lo_ref[p, :, h * tile:(h + 1) * tile] = lo
        return carry

    lax.fori_loop(0, pieces, convert, 0)


def layer_kernel(
    rz, rp, cn, norm,
    order, feat, weight, bias, grad_hidden, hi_any, lo_any,
    hid_out, gf_out, gw_out, gb_out,
    ahi, alo, xall, yfull, zpart, zrecv, c1send, c1recv, c2send, c2recv,
    g1send, g1recv, g2send, g2recv, gall,
    a_sem, x_ss, x_rs, y_ss, y_rs, z_ss, z_rs, c1_ss, c1_rs, c2_ss, c2_rs,
    g1_ss, g1_rs, g2_ss, g2_rs, g3_ss, g3_rs,
):
    row, col = lax.axis_index("row"), lax.axis_index("col")
    zi, pi = row // rp, lax.rem(row, rp)
    fl, nodes = feat.shape
    hl = weight.shape[1]
    fin = weight.shape[0]
    fr = fin // rp

    def zmate(d):
        return (lax.rem(zi + d, rz) * rp + pi, col)

    def pmate(d):
        return (zi * rp + lax.rem(pi + d, rp), col)

    def cmate(d):
        return (row, lax.rem(col + d, cn))

    mates = [zmate(d) for d in range(1, rz)]
    mates += [pmate(d) for d in range(1, rp)]
    mates += [cmate(d) for d in range(1, cn)]

    def remote(src, dst, ss, rs, to):
        return pltpu.make_async_remote_copy(
            src_ref=src, dst_ref=dst, send_sem=ss, recv_sem=rs,
            device_id=to, device_id_type=MESH,
        )

    load_hi = pltpu.make_async_copy(hi_any, ahi, a_sem.at[0])
    load_lo = pltpu.make_async_copy(lo_any, alo, a_sem.at[1])
    load_hi.start()
    load_lo.start()
    barrier = pltpu.get_barrier_semaphore()
    for mate in mates:
        pl.semaphore_signal(barrier, inc=1, device_id=mate, device_id_type=MESH)

    local = order[...] - row * nodes
    pick = (lax.broadcasted_iota(jnp.int32, (nodes, nodes), 0) == local).astype(F32).astype(BF16)
    xall[0, 0] = mm(feat[...], pick, NN).astype(BF16)
    pl.semaphore_wait(barrier, len(mates))

    sent = []

    def go(c):
        c.start()
        sent.append(c)
        return c

    xz = {d: go(remote(xall.at[0, 0], xall.at[d, 0], x_ss.at[d, 0], x_rs.at[d, 0], zmate(d)))
          for d in range(1, rz)}
    xp = {}

    def relay(dz):
        for dp in range(1, rp):
            xp[dz, dp] = go(remote(xall.at[dz, 0], xall.at[dz, dp], x_ss.at[dz, dp],
                                   x_rs.at[dz, dp], pmate(dp)))

    relay(0)
    load_hi.wait()
    load_lo.wait()

    def piece(dz, dp):
        return lax.rem(zi + rz - dz, rz) * rp + lax.rem(pi + rp - dp, rp)

    def term(dz, dp):
        at = piece(dz, dp)
        x = xall[dz, dp]
        return mm(x, ahi[at], NT) + mm(x, alo[at], NT)

    y = term(0, 0)
    for dz in range(1, rz):
        xz[dz].wait_recv()
        relay(dz)
        y = y + term(dz, 0)
    for dz in range(rz):
        for dp in range(1, rp):
            xp[dz, dp].wait_recv()
            y = y + term(dz, dp)

    mine = pl.ds(pl.multiple_of(col * fl, fl), fl)
    yfull[mine, :] = y
    yx = [go(remote(yfull.at[mine], yfull.at[mine], y_ss.at[d], y_rs.at[d], cmate(d)))
          for d in range(1, cn)]
    for c in yx:
        c.wait_recv()
    y_hi, y_lo = split(yfull[...])

    w = weight[...]
    first = lax.broadcasted_iota(jnp.int32, (16, hl), 0) == 0
    bias_rows = jnp.where(first, bias[...].astype(F32), 0.0).astype(BF16)
    pre = mm(w, y_hi, TN) + mm(w, y_lo, TN) + mm(bias_rows, jnp.ones((16, nodes), BF16), TN)
    gate = jax.nn.sigmoid(pre)
    hid_out[...] = (pre * gate).astype(BF16)
    grad_pre = grad_hidden[...].astype(F32) * gate * (1.0 + pre * (1.0 - gate))
    gp_hi, gp_lo = split(grad_pre)

    zpart[...] = mm(w, gp_hi, NN) + mm(w, gp_lo, NN)
    zx = []
    for d in range(1, cn):
        theirs = pl.ds(pl.multiple_of(lax.rem(col + d, cn) * fl, fl), fl)
        zx.append(go(remote(zpart.at[theirs], zrecv.at[d], z_ss.at[d], z_rs.at[d], cmate(d))))

    gw = mm(y_hi, gp_hi, NT) + mm(y_lo, gp_hi, NT) + mm(y_hi, gp_lo, NT)
    ones = jnp.ones((16, nodes), BF16)
    gb = (mm(ones, gp_hi, NT) + mm(ones, gp_lo, NT))[:8]
    for q in range(rp):
        g1send[q, :fr] = gw[q * fr:(q + 1) * fr]
        g1send[q, fr:] = gb
    g1 = [go(remote(g1send.at[lax.rem(pi + d, rp)], g1recv.at[d], g1_ss.at[d], g1_rs.at[d],
                    pmate(d))) for d in range(1, rp)]

    z = zpart[mine, :]
    for d in range(1, cn):
        zx[d - 1].wait_recv()
        z = z + zrecv[d]
    z_hi, z_lo = split(z)
    z_two = jnp.concatenate([z_hi, z_lo], axis=0)

    c1 = {}

    def contribute(d):
        for dp in list(range(1, rp)) + [0]:
            at = lax.rem(zi + d, rz) * rp + lax.rem(pi + dp, rp)
            both = mm(z_two, ahi[at], NN)
            c1send[d, dp] = both[:fl] + both[fl:] + mm(z_hi, alo[at], NN)
            if dp:
                c1[d, dp] = go(remote(c1send.at[d, dp], c1recv.at[d, dp], c1_ss.at[d, dp],
                                      c1_rs.at[d, dp], pmate(dp)))

    def reduced(d):
        total = c1send[d, 0]
        for dp in range(1, rp):
            c1[d, dp].wait_recv()
            total = total + c1recv[d, dp]
        return total

    c2 = {}

    def pass_on(d):
        c2send[d] = reduced(d)
        c2[d] = go(remote(c2send.at[d], c2recv.at[d], c2_ss.at[d], c2_rs.at[d], zmate(d)))

    contribute(1)
    for d in range(2, rz):
        contribute(d)
        pass_on(d - 1)
    contribute(0)
    pass_on(rz - 1)

    part = g1send[pi]
    for d in range(1, rp):
        g1[d - 1].wait_recv()
        part = part + g1recv[d]
    g2send[...] = part
    g2 = [go(remote(g2send, g2recv.at[d], g2_ss.at[d], g2_rs.at[d], zmate(d)))
          for d in range(1, rz)]
    total = reduced(0)
    for d in range(1, rz):
        g2[d - 1].wait_recv()
        part = part + g2recv[d]
    gall[pi] = part[:fr]
    g3 = [go(remote(gall.at[pi], gall.at[pi], g3_ss.at[d], g3_rs.at[d], pmate(d)))
          for d in range(1, rp)]
    gb_out[...] = part[fr:fr + 1] * norm
    for d in range(1, rz):
        c2[d].wait_recv()
        total = total + c2recv[d]
    gf_out[...] = total
    for c in g3:
        c.wait_recv()
    gw_out[...] = gall[...].reshape(fin, hl) * norm
    for c in sent:
        c.wait_send()


def per_device(r, cn, features, order, weight, bias, tiles, coords, counts, grad_hidden):
    rows, slots, tile, _ = tiles.shape
    nodes = order.shape[0]
    fl = features.shape[0]
    fin, hl = weight.shape
    rz = 4 if r % 4 == 0 else 1
    rp = r // rz
    fr = fin // rp
    norm = 1.0 / math.sqrt(nodes * r)
    vmem = pl.BlockSpec(memory_space=pltpu.VMEM)
    smem = pl.BlockSpec(memory_space=pltpu.SMEM)
    anyw = pl.BlockSpec(memory_space=pl.ANY)
    dense = jax.ShapeDtypeStruct((r, nodes, nodes), BF16)
    hi, lo = pl.pallas_call(
        build_kernel,
        out_shape=(dense, dense),
        in_specs=[anyw, smem, smem],
        out_specs=(vmem, vmem),
        scratch_shapes=[
            pltpu.VMEM((rows, slots, tile, tile), BF16),
            pltpu.VMEM((r * rows, nodes, tile), F32),
            pltpu.SemaphoreType.DMA((rows, slots // GROUP)),
        ],
        compiler_params=pltpu.CompilerParams(vmem_limit_bytes=VMEM_LIMIT),
        name="build_dense",
    )(tiles, coords, counts)

    dma = pltpu.SemaphoreType.DMA
    outs = (
        jax.ShapeDtypeStruct((hl, nodes), BF16),
        jax.ShapeDtypeStruct((fl, nodes), F32),
        jax.ShapeDtypeStruct((fin, hl), F32),
        jax.ShapeDtypeStruct((1, hl), F32),
    )
    hidden, gf, gw, gb = pl.pallas_call(
        functools.partial(layer_kernel, rz, rp, cn, norm),
        out_shape=outs,
        in_specs=[vmem] * 5 + [anyw] * 2,
        out_specs=(vmem,) * 4,
        scratch_shapes=[
            pltpu.VMEM((r, nodes, nodes), BF16),
            pltpu.VMEM((r, nodes, nodes), BF16),
            pltpu.VMEM((rz, rp, fl, nodes), BF16),
            pltpu.VMEM((fin, nodes), F32),
            pltpu.VMEM((fin, nodes), F32),
            pltpu.VMEM((cn, fl, nodes), F32),
            pltpu.VMEM((rz, rp, fl, nodes), F32),
            pltpu.VMEM((rz, rp, fl, nodes), F32),
            pltpu.VMEM((rz, fl, nodes), F32),
            pltpu.VMEM((rz, fl, nodes), F32),
            pltpu.VMEM((rp, fr + 8, hl), F32),
            pltpu.VMEM((rp, fr + 8, hl), F32),
            pltpu.VMEM((fr + 8, hl), F32),
            pltpu.VMEM((rz, fr + 8, hl), F32),
            pltpu.VMEM((rp, fr, hl), F32),
            dma((2,)),
            dma((rz, rp)), dma((rz, rp)),
            dma((cn,)), dma((cn,)),
            dma((cn,)), dma((cn,)),
            dma((rz, rp)), dma((rz, rp)),
            dma((rz,)), dma((rz,)),
            dma((rp,)), dma((rp,)),
            dma((rz,)), dma((rz,)),
            dma((rp,)), dma((rp,)),
        ],
        compiler_params=pltpu.CompilerParams(
            collective_id=0, has_side_effects=True, vmem_limit_bytes=VMEM_LIMIT
        ),
        name="layer",
    )(order.reshape(1, nodes), features, weight, bias.reshape(1, hl), grad_hidden, hi, lo)
    return hidden, gf, gw, gb.reshape(hl)


def solution(mesh):
    in_specs = (
        P("col", "row"),
        P("row"),
        P(None, "col"),
        P("col"),
        P("row", None, None, None),
        P("row", None),
        P("row"),
        P("col", "row"),
    )
    out_specs = (P("col", "row"), P("col", "row"), P(None, "col"), P("col"))
    return jax.shard_map(
        functools.partial(per_device, mesh.shape["row"], mesh.shape["col"]),
        mesh=mesh, in_specs=in_specs, out_specs=out_specs, check_vma=False,
    )
```

```python
import functools
import math

import jax
import jax.numpy as jnp
from jax import lax
from jax.experimental import pallas as pl
from jax.experimental.pallas import tpu as pltpu
from jax.sharding import PartitionSpec as P

MESH = pl.DeviceIdType.MESH
F32 = jnp.float32
BF16 = jnp.bfloat16
WIRE = jnp.int16
TOP = 32000.0
GROUP = 8
VMEM_LIMIT = 56 * 1024 * 1024

NN = (((1,), (0,)), ((), ()))
NT = (((1,), (1,)), ((), ()))
TN = (((0,), (0,)), ((), ()))


def mm(a, b, dims):
    return lax.dot_general(a, b, dims, preferred_element_type=F32)


def split(x):
    hi = x.astype(BF16)
    return hi, (x - hi.astype(F32)).astype(BF16)


def encode(x, scale):
    v = jnp.abs(x) * scale
    u = v * lax.rsqrt(v + 1e-30)
    return jnp.round(jnp.where(x < 0, -u, u)).astype(jnp.int32).astype(WIRE)


def decode(code, unit):
    u = code.astype(jnp.int32).astype(F32)
    return u * jnp.abs(u) * unit


def build_kernel(tiles, coords, counts, hi_ref, lo_ref, top_ref, buf, acc, sems):
    rows, slots, tile, _ = buf.shape
    groups = slots // GROUP

    def copy(i, g):
        part = pl.ds(g * GROUP, GROUP)
        return pltpu.make_async_copy(tiles.at[i, part], buf.at[i, part], sems.at[i, g])

    for g in range(groups):
        for i in range(rows):
            @pl.when(counts[i] > g * GROUP)
            def _():
                copy(i, g).start()
    acc[...] = jnp.zeros_like(acc)
    for g in range(groups):
        for i in range(rows):
            live = jnp.clip(counts[i] - g * GROUP, 0, GROUP)

            @pl.when(live > 0)
            def _():
                copy(i, g).wait()

                def add(k, carry):
                    at = g * GROUP + k
                    j = coords[i, at]
                    mine = pl.ds(i * tile, tile)
                    acc[j, mine, :] = acc[j, mine, :] + buf[i, at].astype(F32)
                    return carry

                lax.fori_loop(0, live, add, 0)
    pieces = hi_ref.shape[0]

    def convert(p, top):
        for h in range(rows):
            dense = acc[p * rows + h]
            hi, lo = split(dense)
            squares = jnp.sum(dense * dense, axis=0, keepdims=True)
            top = jnp.maximum(top, jnp.broadcast_to(squares, top.shape))
            hi_ref[p, :, h * tile:(h + 1) * tile] = hi
            lo_ref[p, :, h * tile:(h + 1) * tile] = lo
        return top

    top_ref[...] = lax.fori_loop(0, pieces, convert, jnp.zeros((8, tile), F32))


def layer_kernel(
    rz, rp, cn, norm,
    order, feat, weight, bias, grad_hidden, top, hi_any, lo_any,
    hid_out, gf_out, gw_out, gb_out,
    ahi, alo, xall, yfull, zpart, zrecv, c1send, c1recv, c2send, c2recv,
    g1send, g1recv, g2send, g2recv, gall, s1send, s1recv, s2send, s2recv,
    a_sem, x_ss, x_rs, y_ss, y_rs, z_ss, z_rs, c1_ss, c1_rs, c2_ss, c2_rs,
    g1_ss, g1_rs, g2_ss, g2_rs, g3_ss, g3_rs, s1_ss, s1_rs, s2_ss, s2_rs,
):
    row, col = lax.axis_index("row"), lax.axis_index("col")
    zi, pi = row // rp, lax.rem(row, rp)
    fl, nodes = feat.shape
    hl = weight.shape[1]
    fin = weight.shape[0]
    fr = fin // rp

    def zmate(d):
        return (lax.rem(zi + d, rz) * rp + pi, col)

    def pmate(d):
        return (zi * rp + lax.rem(pi + d, rp), col)

    def cmate(d):
        return (row, lax.rem(col + d, cn))

    mates = [zmate(d) for d in range(1, rz)]
    mates += [pmate(d) for d in range(1, rp)]
    mates += [cmate(d) for d in range(1, cn)]

    def remote(src, dst, ss, rs, to):
        return pltpu.make_async_remote_copy(
            src_ref=src, dst_ref=dst, send_sem=ss, recv_sem=rs,
            device_id=to, device_id_type=MESH,
        )

    load_hi = pltpu.make_async_copy(hi_any, ahi, a_sem.at[0])
    load_lo = pltpu.make_async_copy(lo_any, alo, a_sem.at[1])
    load_hi.start()
    load_lo.start()
    barrier = pltpu.get_barrier_semaphore()
    for mate in mates:
        pl.semaphore_signal(barrier, inc=1, device_id=mate, device_id_type=MESH)

    local = order[...] - row * nodes
    pick = (lax.broadcasted_iota(jnp.int32, (nodes, nodes), 0) == local).astype(F32).astype(BF16)
    xall[0, 0] = mm(feat[...], pick, NN).astype(BF16)
    pl.semaphore_wait(barrier, len(mates))

    sent = []

    def go(c):
        c.start()
        sent.append(c)
        return c

    xz = {d: go(remote(xall.at[0, 0], xall.at[d, 0], x_ss.at[d, 0], x_rs.at[d, 0], zmate(d)))
          for d in range(1, rz)}
    xp = {}

    def relay(dz):
        for dp in range(1, rp):
            xp[dz, dp] = go(remote(xall.at[dz, 0], xall.at[dz, dp], x_ss.at[dz, dp],
                                   x_rs.at[dz, dp], pmate(dp)))

    relay(0)
    load_hi.wait()
    load_lo.wait()

    def piece(dz, dp):
        return lax.rem(zi + rz - dz, rz) * rp + lax.rem(pi + rp - dp, rp)

    def term(dz, dp):
        at = piece(dz, dp)
        x = xall[dz, dp]
        return mm(x, ahi[at], NT) + mm(x, alo[at], NT)

    y = term(0, 0)
    for dz in range(1, rz):
        xz[dz].wait_recv()
        relay(dz)
        y = y + term(dz, 0)
    for dz in range(rz):
        for dp in range(1, rp):
            xp[dz, dp].wait_recv()
            y = y + term(dz, dp)

    mine = pl.ds(pl.multiple_of(col * fl, fl), fl)
    yfull[mine, :] = y
    yx = [go(remote(yfull.at[mine], yfull.at[mine], y_ss.at[d], y_rs.at[d], cmate(d)))
          for d in range(1, cn)]
    for c in yx:
        c.wait_recv()
    y_hi, y_lo = split(yfull[...])

    w = weight[...]
    first = lax.broadcasted_iota(jnp.int32, (16, hl), 0) == 0
    bias_rows = jnp.where(first, bias[...].astype(F32), 0.0).astype(BF16)
    pre = mm(w, y_hi, TN) + mm(w, y_lo, TN) + mm(bias_rows, jnp.ones((16, nodes), BF16), TN)
    gate = jax.nn.sigmoid(pre)
    hid_out[...] = (pre * gate).astype(BF16)
    grad_pre = grad_hidden[...].astype(F32) * gate * (1.0 + pre * (1.0 - gate))
    gp_hi, gp_lo = split(grad_pre)

    zpart[...] = mm(w, gp_hi, NN) + mm(w, gp_lo, NN)
    zx = []
    for d in range(1, cn):
        theirs = pl.ds(pl.multiple_of(lax.rem(col + d, cn) * fl, fl), fl)
        zx.append(go(remote(zpart.at[theirs], zrecv.at[d], z_ss.at[d], z_rs.at[d], cmate(d))))

    gw = mm(y_hi, gp_hi, NT) + mm(y_lo, gp_hi, NT) + mm(y_hi, gp_lo, NT)
    ones = jnp.ones((16, nodes), BF16)
    gb = (mm(ones, gp_hi, NT) + mm(ones, gp_lo, NT))[:8]
    for q in range(rp):
        g1send[q, :fr] = gw[q * fr:(q + 1) * fr]
        g1send[q, fr:] = gb
    g1 = [go(remote(g1send.at[lax.rem(pi + d, rp)], g1recv.at[d], g1_ss.at[d], g1_rs.at[d],
                    pmate(d))) for d in range(1, rp)]

    z = zpart[mine, :]
    for d in range(1, cn):
        zx[d - 1].wait_recv()
        z = z + zrecv[d]
    longest = jnp.max(jnp.sum(z * z, axis=1, keepdims=True), axis=0, keepdims=True)
    bound = jnp.sqrt(longest * jnp.max(top[...], keepdims=True)) + 1e-16
    s1send[...] = jnp.broadcast_to(bound, s1send.shape)
    s1 = [go(remote(s1send, s1recv.at[d], s1_ss.at[d], s1_rs.at[d], pmate(d)))
          for d in range(1, rp)]
    up = TOP * TOP / bound
    z_hi, z_lo = split(z)
    z_two = jnp.concatenate([z_hi, z_lo], axis=0)

    c1 = {}
    kept = {}

    def contribute(d):
        for dp in list(range(1, rp)) + [0]:
            at = lax.rem(zi + d, rz) * rp + lax.rem(pi + dp, rp)
            both = mm(z_two, ahi[at], NN)
            c = both[:fl] + both[fl:] + mm(z_hi, alo[at], NN)
            if dp == 0:
                kept[d] = c
            else:
                c1send[d, dp] = encode(c, up)
                c1[d, dp] = go(remote(c1send.at[d, dp], c1recv.at[d, dp], c1_ss.at[d, dp],
                                      c1_rs.at[d, dp], pmate(dp)))

    def reduced(d):
        total = kept[d]
        for dp in range(1, rp):
            c1[d, dp].wait_recv()
            total = total + decode(c1recv[d, dp], down[dp])
        return total

    c2 = {}

    def pass_on(d):
        c2send[d] = encode(reduced(d), up2)
        c2[d] = go(remote(c2send.at[d], c2recv.at[d], c2_ss.at[d], c2_rs.at[d], zmate(d)))

    contribute(1)
    contribute(2)

    part = g1send[pi]
    for d in range(1, rp):
        g1[d - 1].wait_recv()
        part = part + g1recv[d]
    g2send[...] = part
    g2 = [go(remote(g2send, g2recv.at[d], g2_ss.at[d], g2_rs.at[d], zmate(d)))
          for d in range(1, rz)]
    down = {}
    for d in range(1, rp):
        s1[d - 1].wait_recv()
        down[d] = s1recv[d, :1, :1] * (1.0 / TOP / TOP)
        bound = bound + s1recv[d, :1, :1]
    s2send[...] = jnp.broadcast_to(bound, s2send.shape)
    s2 = [go(remote(s2send, s2recv.at[d], s2_ss.at[d], s2_rs.at[d], zmate(d)))
          for d in range(1, rz)]
    up2 = TOP * TOP / bound

    pass_on(1)
    for d in range(3, rz):
        contribute(d)
        pass_on(d - 1)
    contribute(0)
    for d in range(1, rz):
        g2[d - 1].wait_recv()
        part = part + g2recv[d]
    gall[pi] = part[:fr]
    g3 = [go(remote(gall.at[pi], gall.at[pi], g3_ss.at[d], g3_rs.at[d], pmate(d)))
          for d in range(1, rp)]
    gb_out[...] = part[fr:fr + 1] * norm
    pass_on(rz - 1)
    total = reduced(0)
    for c in g3:
        c.wait_recv()
    gw_out[...] = gall[...].reshape(fin, hl) * norm
    for d in range(1, rz):
        s2[d - 1].wait_recv()
        c2[d].wait_recv()
        total = total + decode(c2recv[d], s2recv[d, :1, :1] * (1.0 / TOP / TOP))
    gf_out[...] = total
    for c in sent:
        c.wait_send()


def hand_over(*refs):
    half = len(refs) // 2
    for source, target in zip(refs[:half], refs[half:]):
        target[...] = source[...]


def per_device(r, cn, features, order, weight, bias, tiles, coords, counts, grad_hidden):
    rows, slots, tile, _ = tiles.shape
    nodes = order.shape[0]
    fl = features.shape[0]
    fin, hl = weight.shape
    rz = 4
    assert r % rz == 0
    rp = r // rz
    fr = fin // rp
    norm = 1.0 / math.sqrt(nodes * r)
    vmem = pl.BlockSpec(memory_space=pltpu.VMEM)
    smem = pl.BlockSpec(memory_space=pltpu.SMEM)
    anyw = pl.BlockSpec(memory_space=pl.ANY)
    dense = jax.ShapeDtypeStruct((r, nodes, nodes), BF16)
    hi, lo, top = pl.pallas_call(
        build_kernel,
        out_shape=(dense, dense, jax.ShapeDtypeStruct((8, tile), F32)),
        in_specs=[anyw, smem, smem],
        out_specs=(vmem, vmem, vmem),
        scratch_shapes=[
            pltpu.VMEM((rows, slots, tile, tile), BF16),
            pltpu.VMEM((r * rows, nodes, tile), F32),
            pltpu.SemaphoreType.DMA((rows, slots // GROUP)),
        ],
        compiler_params=pltpu.CompilerParams(vmem_limit_bytes=VMEM_LIMIT),
        name="build_dense",
    )(tiles, coords, counts)

    dma = pltpu.SemaphoreType.DMA
    outs = (
        jax.ShapeDtypeStruct((hl, nodes), BF16),
        jax.ShapeDtypeStruct((fl, nodes), F32),
        jax.ShapeDtypeStruct((fin, hl), F32),
        jax.ShapeDtypeStruct((1, hl), F32),
    )
    hidden, gf, gw, gb = pl.pallas_call(
        functools.partial(layer_kernel, rz, rp, cn, norm),
        out_shape=outs,
        in_specs=[vmem] * 6 + [anyw] * 2,
        out_specs=(vmem,) * 4,
        scratch_shapes=[
            pltpu.VMEM((r, nodes, nodes), BF16),
            pltpu.VMEM((r, nodes, nodes), BF16),
            pltpu.VMEM((rz, rp, fl, nodes), BF16),
            pltpu.VMEM((fin, nodes), F32),
            pltpu.VMEM((fin, nodes), F32),
            pltpu.VMEM((cn, fl, nodes), F32),
            pltpu.VMEM((rz, rp, fl, nodes), WIRE),
            pltpu.VMEM((rz, rp, fl, nodes), WIRE),
            pltpu.VMEM((rz, fl, nodes), WIRE),
            pltpu.VMEM((rz, fl, nodes), WIRE),
            pltpu.VMEM((rp, fr + 8, hl), F32),
            pltpu.VMEM((rp, fr + 8, hl), F32),
            pltpu.VMEM((fr + 8, hl), F32),
            pltpu.VMEM((rz, fr + 8, hl), F32),
            pltpu.VMEM((rp, fr, hl), F32),
            pltpu.VMEM((8, 128), F32),
            pltpu.VMEM((rp, 8, 128), F32),
            pltpu.VMEM((8, 128), F32),
            pltpu.VMEM((rz, 8, 128), F32),
            dma((2,)),
            dma((rz, rp)), dma((rz, rp)),
            dma((cn,)), dma((cn,)),
            dma((cn,)), dma((cn,)),
            dma((rz, rp)), dma((rz, rp)),
            dma((rz,)), dma((rz,)),
            dma((rp,)), dma((rp,)),
            dma((rz,)), dma((rz,)),
            dma((rp,)), dma((rp,)),
            dma((rp,)), dma((rp,)),
            dma((rz,)), dma((rz,)),
        ],
        compiler_params=pltpu.CompilerParams(
            collective_id=0, has_side_effects=True, vmem_limit_bytes=VMEM_LIMIT
        ),
        name="layer",
    )(order.reshape(1, nodes), features, weight, bias.reshape(1, hl), grad_hidden, top, hi, lo)
    hidden, gf, gw, gb = pl.pallas_call(
        hand_over,
        out_shape=outs,
        in_specs=[vmem] * 4,
        out_specs=(vmem,) * 4,
        name="hand_over",
    )(hidden, gf, gw, gb)
    return hidden, gf, gw, gb.reshape(hl)


def solution(mesh):
    in_specs = (
        P("col", "row"),
        P("row"),
        P(None, "col"),
        P("col"),
        P("row", None, None, None),
        P("row", None),
        P("row"),
        P("col", "row"),
    )
    out_specs = (P("col", "row"), P("col", "row"), P(None, "col"), P("col"))
    return jax.shard_map(
        functools.partial(per_device, mesh.shape["row"], mesh.shape["col"]),
        mesh=mesh, in_specs=in_specs, out_specs=out_specs, check_vma=False,
    )
```

```python
import functools
import math

import jax
import jax.numpy as jnp
from jax import lax
from jax.experimental import pallas as pl
from jax.experimental.pallas import tpu as pltpu
from jax.sharding import PartitionSpec as P

MESH = pl.DeviceIdType.MESH
F32 = jnp.float32
BF16 = jnp.bfloat16
WIRE = jnp.int16
TOP = 32000.0
VMEM_LIMIT = 56 * 1024 * 1024

NN = (((1,), (0,)), ((), ()))
NT = (((1,), (1,)), ((), ()))
TN = (((0,), (0,)), ((), ()))


def mm(a, b, dims):
    return lax.dot_general(a, b, dims, preferred_element_type=F32)


def split(x):
    hi = x.astype(BF16)
    return hi, (x - hi.astype(F32)).astype(BF16)


def encode(x, scale):
    v = jnp.abs(x) * scale
    u = v * lax.rsqrt(v + 1e-30)
    return jnp.round(jnp.where(x < 0, -u, u)).astype(jnp.int32).astype(WIRE)


def decode(code, unit):
    u = code.astype(jnp.int32).astype(F32)
    return u * jnp.abs(u) * unit


def slot_table(coords, count):
    slots = coords.shape[1]
    sub = lax.broadcasted_iota(jnp.int32, (slots, slots), 0)
    lane = lax.broadcasted_iota(jnp.int32, (slots, slots), 1)
    dead = 1 << 12
    key = jnp.where(lane < count, jnp.broadcast_to(coords, (slots, slots)), dead)
    flip = jnp.sum(jnp.where(sub == lane, key, 0), axis=1, keepdims=True)
    same = (key == flip) & (lane < sub)
    ahead = jnp.sum(jnp.where((key < flip) | same, 1, 0), axis=1, keepdims=True)
    keep = jnp.minimum(jnp.sum(jnp.where(same, 1, 0), axis=1, keepdims=True), 1)
    place = lax.broadcasted_iota(jnp.int32, (slots, 128), 1)
    slot = lax.broadcasted_iota(jnp.int32, (slots, 128), 0)
    match = ahead == place

    def down(x):
        return jnp.sum(x, axis=0, keepdims=True)

    order = down(jnp.where(match, slot, 0))
    goes_on = down(jnp.where(match, keep, 0))
    last = jnp.maximum(down(jnp.where(flip <= place, 1, 0)) - 1, 0)
    named = jnp.minimum(down(jnp.where(flip == place, 1, 0)), 1)
    return [order, goes_on, last, named]


def layer_kernel(
    rz, rp, cn, norm,
    order, feat, weight, bias, grad_hidden, coords, counts, tiles,
    hid_out, gf_out, gw_out, gb_out,
    buf, run, table, places, ahi, alo, xall, yfull, zpart, zrecv, c1send, c1recv, c2send, c2recv,
    g1send, g1recv, g2send, g2recv, gall, s1send, s1recv, s2send, s2recv,
    a_sem, x_ss, x_rs, y_ss, y_rs, z_ss, z_rs, c1_ss, c1_rs, c2_ss, c2_rs,
    g1_ss, g1_rs, g2_ss, g2_rs, g3_ss, g3_rs, s1_ss, s1_rs, s2_ss, s2_rs,
):
    row, col = lax.axis_index("row"), lax.axis_index("col")
    zi, pi = row // rp, lax.rem(row, rp)
    fl, nodes = feat.shape
    hl = weight.shape[1]
    fin = weight.shape[0]
    fr = fin // rp

    def zmate(d):
        return (lax.rem(zi + d, rz) * rp + pi, col)

    def pmate(d):
        return (zi * rp + lax.rem(pi + d, rp), col)

    def cmate(d):
        return (row, lax.rem(col + d, cn))

    mates = [zmate(d) for d in range(1, rz)]
    mates += [pmate(d) for d in range(1, rp)]
    mates += [cmate(d) for d in range(1, cn)]

    def remote(src, dst, ss, rs, to):
        return pltpu.make_async_remote_copy(
            src_ref=src, dst_ref=dst, send_sem=ss, recv_sem=rs,
            device_id=to, device_id_type=MESH,
        )

    rows, slots, tile, _ = buf.shape
    loads = [pltpu.make_async_copy(tiles.at[i], buf.at[i], a_sem.at[i]) for i in range(rows)]
    for c in loads:
        c.start()
    barrier = pltpu.get_barrier_semaphore()
    for mate in mates:
        pl.semaphore_signal(barrier, inc=1, device_id=mate, device_id_type=MESH)

    lines = []
    for i in range(rows):
        lines += slot_table(coords[i:i + 1, :], counts[i])
    table[...] = jnp.concatenate(lines, axis=0)
    to_places = pltpu.make_async_copy(table, places, a_sem.at[rows])
    to_places.start()

    local = order[...] - row * nodes
    pick = (lax.broadcasted_iota(jnp.int32, (nodes, nodes), 0) == local).astype(F32).astype(BF16)
    xall[0, 0] = mm(feat[...], pick, NN).astype(BF16)
    pl.semaphore_wait(barrier, len(mates))

    sent = []

    def go(c):
        c.start()
        sent.append(c)
        return c

    xz = {d: go(remote(xall.at[0, 0], xall.at[d, 0], x_ss.at[d, 0], x_rs.at[d, 0], zmate(d)))
          for d in range(1, rz)}
    xp = {}

    def relay(dz):
        for dp in range(1, rp):
            xp[dz, dp] = go(remote(xall.at[dz, 0], xall.at[dz, dp], x_ss.at[dz, dp],
                                   x_rs.at[dz, dp], pmate(dp)))

    relay(0)
    to_places.wait()
    for c in loads:
        c.wait()

    def add(s, sums):
        new = []
        for i in range(rows):
            keep = places[4 * i + 1, s].astype(F32)
            total = sums[i] * keep + buf[i, jnp.clip(places[4 * i, s], 0, slots - 1)].astype(F32)
            run[i, s] = total
            new.append(total)
        return tuple(new)

    sums = tuple(jnp.zeros((tile, tile), F32) for _ in range(rows))
    near = [1, 3, 2]
    step = slots // 4
    for n in range(4):
        sums = lax.fori_loop(n * step, (n + 1) * step, add, sums)
        if n < 3:
            xz[near[n]].wait_recv()
            relay(near[n])

    def place(p, top):
        for h in range(rows):
            squares = jnp.zeros((1, tile), F32)
            for i in range(rows):
                j = p * rows + h
                named = places[4 * i + 3, j].astype(F32)
                dense = run[i, jnp.clip(places[4 * i + 2, j], 0, slots - 1)] * named
                hi, lo = split(dense)
                ahi[p, i * tile:(i + 1) * tile, h * tile:(h + 1) * tile] = hi
                alo[p, i * tile:(i + 1) * tile, h * tile:(h + 1) * tile] = lo
                squares = squares + jnp.sum(dense * dense, axis=0, keepdims=True)
            top = jnp.maximum(top, squares)
        return top

    top = lax.fori_loop(0, rz * rp, place, jnp.zeros((1, tile), F32))

    def piece(dz, dp):
        return lax.rem(zi + rz - dz, rz) * rp + lax.rem(pi + rp - dp, rp)

    def term(dz, dp):
        at = piece(dz, dp)
        x = xall[dz, dp]
        return mm(x, ahi[at], NT) + mm(x, alo[at], NT)

    y = term(0, 0)
    for dz in near:
        y = y + term(dz, 0)
    for dz in [0] + near:
        for dp in range(1, rp):
            xp[dz, dp].wait_recv()
            y = y + term(dz, dp)

    mine = pl.ds(pl.multiple_of(col * fl, fl), fl)
    yfull[mine, :] = y
    yx = [go(remote(yfull.at[mine], yfull.at[mine], y_ss.at[d], y_rs.at[d], cmate(d)))
          for d in range(1, cn)]
    for c in yx:
        c.wait_recv()
    y_hi, y_lo = split(yfull[...])

    w = weight[...]
    first = lax.broadcasted_iota(jnp.int32, (16, hl), 0) == 0
    bias_rows = jnp.where(first, bias[...].astype(F32), 0.0).astype(BF16)
    pre = mm(w, y_hi, TN) + mm(w, y_lo, TN) + mm(bias_rows, jnp.ones((16, nodes), BF16), TN)
    gate = jax.nn.sigmoid(pre)
    hid_out[...] = (pre * gate).astype(BF16)
    grad_pre = grad_hidden[...].astype(F32) * gate * (1.0 + pre * (1.0 - gate))
    gp_hi, gp_lo = split(grad_pre)

    zpart[...] = mm(w, gp_hi, NN) + mm(w, gp_lo, NN)
    zx = []
    for d in range(1, cn):
        theirs = pl.ds(pl.multiple_of(lax.rem(col + d, cn) * fl, fl), fl)
        zx.append(go(remote(zpart.at[theirs], zrecv.at[d], z_ss.at[d], z_rs.at[d], cmate(d))))

    gw = mm(y_hi, gp_hi, NT) + mm(y_lo, gp_hi, NT) + mm(y_hi, gp_lo, NT)
    ones = jnp.ones((16, nodes), BF16)
    gb = (mm(ones, gp_hi, NT) + mm(ones, gp_lo, NT))[:8]
    for q in range(rp):
        g1send[q, :fr] = gw[q * fr:(q + 1) * fr]
        g1send[q, fr:] = gb
    g1 = [go(remote(g1send.at[lax.rem(pi + d, rp)], g1recv.at[d], g1_ss.at[d], g1_rs.at[d],
                    pmate(d))) for d in range(1, rp)]

    z = zpart[mine, :]
    for d in range(1, cn):
        zx[d - 1].wait_recv()
        z = z + zrecv[d]
    longest = jnp.max(jnp.sum(z * z, axis=1, keepdims=True), axis=0, keepdims=True)
    bound = jnp.sqrt(longest * jnp.max(top, keepdims=True)) + 1e-16
    s1send[...] = jnp.broadcast_to(bound, s1send.shape)
    s1 = [go(remote(s1send, s1recv.at[d], s1_ss.at[d], s1_rs.at[d], pmate(d)))
          for d in range(1, rp)]
    up = TOP * TOP / bound
    z_hi, z_lo = split(z)
    z_two = jnp.concatenate([z_hi, z_lo], axis=0)

    c1 = {}
    kept = {}

    def contribute(d):
        for dp in list(range(1, rp)) + [0]:
            at = lax.rem(zi + d, rz) * rp + lax.rem(pi + dp, rp)
            both = mm(z_two, ahi[at], NN)
            c = both[:fl] + both[fl:] + mm(z_hi, alo[at], NN)
            if dp == 0:
                kept[d] = c
            else:
                c1send[d, dp] = encode(c, up)
                c1[d, dp] = go(remote(c1send.at[d, dp], c1recv.at[d, dp], c1_ss.at[d, dp],
                                      c1_rs.at[d, dp], pmate(dp)))

    def reduced(d):
        total = kept[d]
        for dp in range(1, rp):
            c1[d, dp].wait_recv()
            total = total + decode(c1recv[d, dp], down[dp])
        return total

    c2 = {}

    def pass_on(d):
        c2send[d] = encode(reduced(d), up2)
        c2[d] = go(remote(c2send.at[d], c2recv.at[d], c2_ss.at[d], c2_rs.at[d], zmate(d)))

    contribute(1)
    contribute(2)

    part = g1send[pi]
    for d in range(1, rp):
        g1[d - 1].wait_recv()
        part = part + g1recv[d]
    g2send[...] = part
    g2 = [go(remote(g2send, g2recv.at[d], g2_ss.at[d], g2_rs.at[d], zmate(d)))
          for d in range(1, rz)]
    down = {}
    for d in range(1, rp):
        s1[d - 1].wait_recv()
        down[d] = s1recv[d, :1, :1] * (1.0 / TOP / TOP)
        bound = bound + s1recv[d, :1, :1]
    s2send[...] = jnp.broadcast_to(bound, s2send.shape)
    s2 = [go(remote(s2send, s2recv.at[d], s2_ss.at[d], s2_rs.at[d], zmate(d)))
          for d in range(1, rz)]
    up2 = TOP * TOP / bound

    pass_on(1)
    for d in range(3, rz):
        contribute(d)
        pass_on(d - 1)
    contribute(0)
    for d in range(1, rz):
        g2[d - 1].wait_recv()
        part = part + g2recv[d]
    gall[pi] = part[:fr]
    g3 = [go(remote(gall.at[pi], gall.at[pi], g3_ss.at[d], g3_rs.at[d], pmate(d)))
          for d in range(1, rp)]
    gb_out[...] = part[fr:fr + 1] * norm
    pass_on(rz - 1)
    total = reduced(0)
    for c in g3:
        c.wait_recv()
    gw_out[...] = gall[...].reshape(fin, hl) * norm
    for d in range(1, rz):
        s2[d - 1].wait_recv()
        c2[d].wait_recv()
        total = total + decode(c2recv[d], s2recv[d, :1, :1] * (1.0 / TOP / TOP))
    gf_out[...] = total
    for c in sent:
        c.wait_send()


def hand_over(*refs):
    half = len(refs) // 2
    for source, target in zip(refs[:half], refs[half:]):
        target[...] = source[...]


def per_device(r, cn, features, order, weight, bias, tiles, coords, counts, grad_hidden):
    rows, slots, tile, _ = tiles.shape
    nodes = order.shape[0]
    fl = features.shape[0]
    fin, hl = weight.shape
    rz = 4
    assert r % rz == 0 and slots % 4 == 0 and r * rows <= 128
    rp = r // rz
    fr = fin // rp
    norm = 1.0 / math.sqrt(nodes * r)
    vmem = pl.BlockSpec(memory_space=pltpu.VMEM)
    smem = pl.BlockSpec(memory_space=pltpu.SMEM)
    anyw = pl.BlockSpec(memory_space=pl.ANY)
    dma = pltpu.SemaphoreType.DMA
    outs = (
        jax.ShapeDtypeStruct((hl, nodes), BF16),
        jax.ShapeDtypeStruct((fl, nodes), F32),
        jax.ShapeDtypeStruct((fin, hl), F32),
        jax.ShapeDtypeStruct((1, hl), F32),
    )
    hidden, gf, gw, gb = pl.pallas_call(
        functools.partial(layer_kernel, rz, rp, cn, norm),
        out_shape=outs,
        in_specs=[vmem] * 6 + [smem, anyw],
        out_specs=(vmem,) * 4,
        scratch_shapes=[
            pltpu.VMEM((rows, slots, tile, tile), BF16),
            pltpu.VMEM((rows, slots, tile, tile), F32),
            pltpu.VMEM((4 * rows, 128), jnp.int32),
            pltpu.SMEM((4 * rows, 128), jnp.int32),
            pltpu.VMEM((r, nodes, nodes), BF16),
            pltpu.VMEM((r, nodes, nodes), BF16),
            pltpu.VMEM((rz, rp, fl, nodes), BF16),
            pltpu.VMEM((fin, nodes), F32),
            pltpu.VMEM((fin, nodes), F32),
            pltpu.VMEM((cn, fl, nodes), F32),
            pltpu.VMEM((rz, rp, fl, nodes), WIRE),
            pltpu.VMEM((rz, rp, fl, nodes), WIRE),
            pltpu.VMEM((rz, fl, nodes), WIRE),
            pltpu.VMEM((rz, fl, nodes), WIRE),
            pltpu.VMEM((rp, fr + 8, hl), F32),
            pltpu.VMEM((rp, fr + 8, hl), F32),
            pltpu.VMEM((fr + 8, hl), F32),
            pltpu.VMEM((rz, fr + 8, hl), F32),
            pltpu.VMEM((rp, fr, hl), F32),
            pltpu.VMEM((8, 128), F32),
            pltpu.VMEM((rp, 8, 128), F32),
            pltpu.VMEM((8, 128), F32),
            pltpu.VMEM((rz, 8, 128), F32),
            dma((rows + 1,)),
            dma((rz, rp)), dma((rz, rp)),
            dma((cn,)), dma((cn,)),
            dma((cn,)), dma((cn,)),
            dma((rz, rp)), dma((rz, rp)),
            dma((rz,)), dma((rz,)),
            dma((rp,)), dma((rp,)),
            dma((rz,)), dma((rz,)),
            dma((rp,)), dma((rp,)),
            dma((rp,)), dma((rp,)),
            dma((rz,)), dma((rz,)),
        ],
        compiler_params=pltpu.CompilerParams(
            collective_id=0, has_side_effects=True, vmem_limit_bytes=VMEM_LIMIT
        ),
        name="layer",
    )(order.reshape(1, nodes), features, weight, bias.reshape(1, hl), grad_hidden, coords, counts, tiles)
    hidden, gf, gw, gb = pl.pallas_call(
        hand_over,
        out_shape=outs,
        in_specs=[vmem] * 4,
        out_specs=(vmem,) * 4,
        name="hand_over",
    )(hidden, gf, gw, gb)
    return hidden, gf, gw, gb.reshape(hl)


def solution(mesh):
    in_specs = (
        P("col", "row"),
        P("row"),
        P(None, "col"),
        P("col"),
        P("row", None, None, None),
        P("row", None),
        P("row"),
        P("col", "row"),
    )
    out_specs = (P("col", "row"), P("col", "row"), P(None, "col"), P("col"))
    return jax.shard_map(
        functools.partial(per_device, mesh.shape["row"], mesh.shape["col"]),
        mesh=mesh, in_specs=in_specs, out_specs=out_specs, check_vma=False,
    )
```

```python
import functools
import math

import jax
import jax.numpy as jnp
from jax import lax
from jax.experimental import pallas as pl
from jax.experimental.pallas import tpu as pltpu
from jax.sharding import PartitionSpec as P

MESH = pl.DeviceIdType.MESH
F32 = jnp.float32
BF16 = jnp.bfloat16
WIRE = jnp.int16
TOP = 32000.0
VMEM_LIMIT = 56 * 1024 * 1024

NN = (((1,), (0,)), ((), ()))
NT = (((1,), (1,)), ((), ()))
TN = (((0,), (0,)), ((), ()))


def mm(a, b, dims):
    return lax.dot_general(a, b, dims, preferred_element_type=F32)


def split(x):
    hi = x.astype(BF16)
    return hi, (x - hi.astype(F32)).astype(BF16)


def encode(x, scale):
    v = jnp.abs(x) * scale
    u = v * lax.rsqrt(v + 1e-30)
    return jnp.round(jnp.where(x < 0, -u, u)).astype(jnp.int32).astype(WIRE)


def decode(code, unit):
    u = code.astype(jnp.int32).astype(F32)
    return u * jnp.abs(u) * unit


def slot_table(coords, count):
    slots = coords.shape[1]
    sub = lax.broadcasted_iota(jnp.int32, (slots, slots), 0)
    lane = lax.broadcasted_iota(jnp.int32, (slots, slots), 1)
    dead = 1 << 12
    key = jnp.where(lane < count, jnp.broadcast_to(coords, (slots, slots)), dead)
    flip = jnp.sum(jnp.where(sub == lane, key, 0), axis=1, keepdims=True)
    same = (key == flip) & (lane < sub)
    ahead = jnp.sum(jnp.where((key < flip) | same, 1, 0), axis=1, keepdims=True)
    keep = jnp.minimum(jnp.sum(jnp.where(same, 1, 0), axis=1, keepdims=True), 1)
    place = lax.broadcasted_iota(jnp.int32, (slots, 128), 1)
    slot = lax.broadcasted_iota(jnp.int32, (slots, 128), 0)
    match = ahead == place

    def down(x):
        return jnp.sum(x, axis=0, keepdims=True)

    order = down(jnp.where(match, slot, 0))
    goes_on = down(jnp.where(match, keep, 0))
    last = jnp.maximum(down(jnp.where(flip <= place, 1, 0)) - 1, 0)
    named = jnp.minimum(down(jnp.where(flip == place, 1, 0)), 1)
    return [order, goes_on, last, named]


def layer_kernel(
    rz, rp, cn, norm,
    order, feat, weight, bias, grad_hidden, coords, counts, tiles,
    hid_out, gf_out, gw_out, gb_out,
    buf, run, table, places, ahi, alo, xall, yfull, wall, hall, c1send, c1recv, c2send, c2recv,
    g1send, g1recv, g2send, g2recv, gall, s1send, s1recv, s2send, s2recv,
    a_sem, x_ss, x_rs, y_ss, y_rs, w_ss, w_rs, h_ss, h_rs, c1_ss, c1_rs, c2_ss, c2_rs,
    g1_ss, g1_rs, g2_ss, g2_rs, g3_ss, g3_rs, s1_ss, s1_rs, s2_ss, s2_rs,
):
    row, col = lax.axis_index("row"), lax.axis_index("col")
    zi, pi = row // rp, lax.rem(row, rp)
    fl, nodes = feat.shape
    hl = weight.shape[1]
    fin = weight.shape[0]
    fr = fin // rp

    def zmate(d):
        return (lax.rem(zi + d, rz) * rp + pi, col)

    def pmate(d):
        return (zi * rp + lax.rem(pi + d, rp), col)

    def cmate(d):
        return (row, lax.rem(col + d, cn))

    mates = [zmate(d) for d in range(1, rz)]
    mates += [pmate(d) for d in range(1, rp)]
    mates += [cmate(d) for d in range(1, cn)]

    def remote(src, dst, ss, rs, to):
        return pltpu.make_async_remote_copy(
            src_ref=src, dst_ref=dst, send_sem=ss, recv_sem=rs,
            device_id=to, device_id_type=MESH,
        )

    rows, slots, tile, _ = buf.shape
    loads = [pltpu.make_async_copy(tiles.at[i], buf.at[i], a_sem.at[i]) for i in range(rows)]
    for c in loads:
        c.start()
    barrier = pltpu.get_barrier_semaphore()
    for mate in mates:
        pl.semaphore_signal(barrier, inc=1, device_id=mate, device_id_type=MESH)

    lines = []
    for i in range(rows):
        lines += slot_table(coords[i:i + 1, :], counts[i])
    table[...] = jnp.concatenate(lines, axis=0)
    to_places = pltpu.make_async_copy(table, places, a_sem.at[rows])
    to_places.start()

    local = order[...] - row * nodes
    pick = (lax.broadcasted_iota(jnp.int32, (nodes, nodes), 0) == local).astype(F32).astype(BF16)
    xall[0, 0] = mm(feat[...], pick, NN).astype(BF16)
    first = lax.broadcasted_iota(jnp.int32, (16, hl), 0) == 0
    wall[0, :fin, :] = weight[...]
    wall[0, fin:, :] = jnp.where(first, bias[...].astype(F32), 0.0).astype(BF16)
    pl.semaphore_wait(barrier, len(mates))

    sent = []

    def go(c):
        c.start()
        sent.append(c)
        return c

    xz = {d: go(remote(xall.at[0, 0], xall.at[d, 0], x_ss.at[d, 0], x_rs.at[d, 0], zmate(d)))
          for d in range(1, rz)}
    xp = {}

    def relay(dz):
        for dp in range(1, rp):
            xp[dz, dp] = go(remote(xall.at[dz, 0], xall.at[dz, dp], x_ss.at[dz, dp],
                                   x_rs.at[dz, dp], pmate(dp)))

    relay(0)
    wx = [go(remote(wall.at[0], wall.at[d], w_ss.at[d], w_rs.at[d], cmate(d)))
          for d in range(1, cn)]
    hx = [go(remote(grad_hidden, hall.at[d], h_ss.at[d], h_rs.at[d], cmate(d)))
          for d in range(1, cn)]
    to_places.wait()
    for c in loads:
        c.wait()

    def add(s, sums):
        new = []
        for i in range(rows):
            keep = places[4 * i + 1, s].astype(F32)
            total = sums[i] * keep + buf[i, jnp.clip(places[4 * i, s], 0, slots - 1)].astype(F32)
            run[i, s] = total
            new.append(total)
        return tuple(new)

    sums = tuple(jnp.zeros((tile, tile), F32) for _ in range(rows))
    near = [1, 3, 2]
    step = slots // 4
    for n in range(4):
        sums = lax.fori_loop(n * step, (n + 1) * step, add, sums, unroll=4)
        if n < 3:
            xz[near[n]].wait_recv()
            relay(near[n])

    def place(p, top):
        for h in range(rows):
            squares = jnp.zeros((1, tile), F32)
            for i in range(rows):
                j = p * rows + h
                named = places[4 * i + 3, j].astype(F32)
                dense = run[i, jnp.clip(places[4 * i + 2, j], 0, slots - 1)] * named
                hi, lo = split(dense)
                ahi[p, i * tile:(i + 1) * tile, h * tile:(h + 1) * tile] = hi
                alo[p, i * tile:(i + 1) * tile, h * tile:(h + 1) * tile] = lo
                squares = squares + jnp.sum(dense * dense, axis=0, keepdims=True)
            top = jnp.maximum(top, squares)
        return top

    def piece(dz, dp):
        return lax.rem(zi + rz - dz, rz) * rp + lax.rem(pi + rp - dp, rp)

    order_in = [(0, 0)] + [(dz, 0) for dz in near]
    order_in += [(dz, dp) for dz in [0] + near for dp in range(1, rp)]
    top = jnp.zeros((1, tile), F32)
    y = jnp.zeros((fl, nodes), F32)
    for dz, dp in order_in:
        at = piece(dz, dp)
        top = place(at, top)
        if dp:
            xp[dz, dp].wait_recv()
        x = xall[dz, dp]
        y = y + mm(x, ahi[at], NT) + mm(x, alo[at], NT)

    mine = pl.ds(pl.multiple_of(col * fl, fl), fl)
    yfull[mine, :] = y
    yx = [go(remote(yfull.at[mine], yfull.at[mine], y_ss.at[d], y_rs.at[d], cmate(d)))
          for d in range(1, cn)]
    for c in yx:
        c.wait_recv()
    for c in wx + hx:
        c.wait_recv()
    y_hi, y_lo = split(yfull[...])
    ones = jnp.ones((16, nodes), BF16)
    y_ext = jnp.concatenate([y_hi, ones], axis=0)

    z = jnp.zeros((fl, nodes), F32)
    for d in range(cn):
        pre = mm(wall[d], y_ext, TN) + mm(wall[d, :fin, :], y_lo, TN)
        gate = jax.nn.sigmoid(pre)
        cotangent = grad_hidden[...] if d == 0 else hall[d]
        grad_pre = cotangent.astype(F32) * gate * (1.0 + pre * (1.0 - gate))
        part_hi, part_lo = split(grad_pre)
        z = z + mm(wall[d, mine, :], part_hi, NN) + mm(wall[d, mine, :], part_lo, NN)
        if d == 0:
            hid_out[...] = (pre * gate).astype(BF16)
            gp_hi, gp_lo = part_hi, part_lo

    longest = jnp.max(jnp.sum(z * z, axis=1, keepdims=True), axis=0, keepdims=True)
    bound = jnp.sqrt(longest * jnp.max(top, keepdims=True)) + 1e-16
    s1send[...] = jnp.broadcast_to(bound, s1send.shape)
    s1 = [go(remote(s1send, s1recv.at[d], s1_ss.at[d], s1_rs.at[d], pmate(d)))
          for d in range(1, rp)]
    up = TOP * TOP / bound
    z_hi, z_lo = split(z)
    z_two = jnp.concatenate([z_hi, z_lo], axis=0)

    c1 = {}
    kept = {}

    def contribute(d):
        for dp in list(range(1, rp)) + [0]:
            at = lax.rem(zi + d, rz) * rp + lax.rem(pi + dp, rp)
            both = mm(z_two, ahi[at], NN)
            c = both[:fl] + both[fl:] + mm(z_hi, alo[at], NN)
            if dp == 0:
                kept[d] = c
            else:
                c1send[d, dp] = encode(c, up)
                c1[d, dp] = go(remote(c1send.at[d, dp], c1recv.at[d, dp], c1_ss.at[d, dp],
                                      c1_rs.at[d, dp], pmate(dp)))

    def reduced(d):
        total = kept[d]
        for dp in range(1, rp):
            c1[d, dp].wait_recv()
            total = total + decode(c1recv[d, dp], down[dp])
        return total

    c2 = {}

    def pass_on(d):
        c2send[d] = encode(reduced(d), up2)
        c2[d] = go(remote(c2send.at[d], c2recv.at[d], c2_ss.at[d], c2_rs.at[d], zmate(d)))

    contribute(1)

    gw = mm(y_ext, gp_hi, NT) + mm(y_ext, gp_lo, NT)
    gb = gw[fin:fin + 8]
    gw = gw[:fin] + mm(y_lo, gp_hi, NT)
    for q in range(rp):
        g1send[q, :fr] = gw[q * fr:(q + 1) * fr]
        g1send[q, fr:] = gb
    g1 = [go(remote(g1send.at[lax.rem(pi + d, rp)], g1recv.at[d], g1_ss.at[d], g1_rs.at[d],
                    pmate(d))) for d in range(1, rp)]
    contribute(2)

    down = {}
    for d in range(1, rp):
        s1[d - 1].wait_recv()
        down[d] = s1recv[d, :1, :1] * (1.0 / TOP / TOP)
        bound = bound + s1recv[d, :1, :1]
    s2send[...] = jnp.broadcast_to(bound, s2send.shape)
    s2 = [go(remote(s2send, s2recv.at[d], s2_ss.at[d], s2_rs.at[d], zmate(d)))
          for d in range(1, rz)]
    up2 = TOP * TOP / bound

    pass_on(1)
    for d in range(3, rz):
        contribute(d)
        pass_on(d - 1)
    part = g1send[pi]
    for d in range(1, rp):
        g1[d - 1].wait_recv()
        part = part + g1recv[d]
    g2send[...] = part
    g2 = [go(remote(g2send, g2recv.at[d], g2_ss.at[d], g2_rs.at[d], zmate(d)))
          for d in range(1, rz)]
    contribute(0)
    for d in range(1, rz):
        g2[d - 1].wait_recv()
        part = part + g2recv[d]
    gall[pi] = part[:fr]
    g3 = [go(remote(gall.at[pi], gall.at[pi], g3_ss.at[d], g3_rs.at[d], pmate(d)))
          for d in range(1, rp)]
    gb_out[...] = part[fr:fr + 1] * norm
    pass_on(rz - 1)
    total = reduced(0)
    for c in g3:
        c.wait_recv()
    gw_out[...] = gall[...].reshape(fin, hl) * norm
    for d in range(1, rz):
        s2[d - 1].wait_recv()
        c2[d].wait_recv()
        total = total + decode(c2recv[d], s2recv[d, :1, :1] * (1.0 / TOP / TOP))
    gf_out[...] = total
    for c in sent:
        c.wait_send()


def hand_over(*refs):
    sems = refs[-1]
    half = len(refs) // 2
    copies = [pltpu.make_async_copy(refs[n], refs[half + n], sems.at[n]) for n in range(half)]
    for c in copies:
        c.start()
    for c in copies:
        c.wait()


def per_device(r, cn, features, order, weight, bias, tiles, coords, counts, grad_hidden):
    rows, slots, tile, _ = tiles.shape
    nodes = order.shape[0]
    fl = features.shape[0]
    fin, hl = weight.shape
    rz = 4
    assert r % rz == 0 and slots % 4 == 0 and r * rows <= 128
    rp = r // rz
    fr = fin // rp
    norm = 1.0 / math.sqrt(nodes * r)
    vmem = pl.BlockSpec(memory_space=pltpu.VMEM)
    smem = pl.BlockSpec(memory_space=pltpu.SMEM)
    anyw = pl.BlockSpec(memory_space=pl.ANY)
    dma = pltpu.SemaphoreType.DMA
    outs = (
        jax.ShapeDtypeStruct((hl, nodes), BF16),
        jax.ShapeDtypeStruct((fl, nodes), F32),
        jax.ShapeDtypeStruct((fin, hl), F32),
        jax.ShapeDtypeStruct((1, hl), F32),
    )
    hidden, gf, gw, gb = pl.pallas_call(
        functools.partial(layer_kernel, rz, rp, cn, norm),
        out_shape=outs,
        in_specs=[vmem] * 6 + [smem, anyw],
        out_specs=(vmem,) * 4,
        scratch_shapes=[
            pltpu.VMEM((rows, slots, tile, tile), BF16),
            pltpu.VMEM((rows, slots, tile, tile), F32),
            pltpu.VMEM((4 * rows, 128), jnp.int32),
            pltpu.SMEM((4 * rows, 128), jnp.int32),
            pltpu.VMEM((r, nodes, nodes), BF16),
            pltpu.VMEM((r, nodes, nodes), BF16),
            pltpu.VMEM((rz, rp, fl, nodes), BF16),
            pltpu.VMEM((fin, nodes), F32),
            pltpu.VMEM((cn, fin + 16, hl), BF16),
            pltpu.VMEM((cn, hl, nodes), BF16),
            pltpu.VMEM((rz, rp, fl, nodes), WIRE),
            pltpu.VMEM((rz, rp, fl, nodes), WIRE),
            pltpu.VMEM((rz, fl, nodes), WIRE),
            pltpu.VMEM((rz, fl, nodes), WIRE),
            pltpu.VMEM((rp, fr + 8, hl), F32),
            pltpu.VMEM((rp, fr + 8, hl), F32),
            pltpu.VMEM((fr + 8, hl), F32),
            pltpu.VMEM((rz, fr + 8, hl), F32),
            pltpu.VMEM((rp, fr, hl), F32),
            pltpu.VMEM((8, 128), F32),
            pltpu.VMEM((rp, 8, 128), F32),
            pltpu.VMEM((8, 128), F32),
            pltpu.VMEM((rz, 8, 128), F32),
            dma((rows + 1,)),
            dma((rz, rp)), dma((rz, rp)),
            dma((cn,)), dma((cn,)),
            dma((cn,)), dma((cn,)),
            dma((cn,)), dma((cn,)),
            dma((rz, rp)), dma((rz, rp)),
            dma((rz,)), dma((rz,)),
            dma((rp,)), dma((rp,)),
            dma((rz,)), dma((rz,)),
            dma((rp,)), dma((rp,)),
            dma((rp,)), dma((rp,)),
            dma((rz,)), dma((rz,)),
        ],
        compiler_params=pltpu.CompilerParams(
            collective_id=0, has_side_effects=True, vmem_limit_bytes=VMEM_LIMIT
        ),
        name="layer",
    )(order.reshape(1, nodes), features, weight, bias.reshape(1, hl), grad_hidden, coords, counts, tiles)
    hidden, gf, gw, gb = pl.pallas_call(
        hand_over,
        out_shape=outs,
        in_specs=[anyw] * 4,
        out_specs=(anyw,) * 4,
        scratch_shapes=[dma((4,))],
        name="hand_over",
    )(hidden, gf, gw, gb)
    return hidden, gf, gw, gb.reshape(hl)


def solution(mesh):
    in_specs = (
        P("col", "row"),
        P("row"),
        P(None, "col"),
        P("col"),
        P("row", None, None, None),
        P("row", None),
        P("row"),
        P("col", "row"),
    )
    out_specs = (P("col", "row"), P("col", "row"), P(None, "col"), P("col"))
    return jax.shard_map(
        functools.partial(per_device, mesh.shape["row"], mesh.shape["col"]),
        mesh=mesh, in_specs=in_specs, out_specs=out_specs, check_vma=False,
    )
```

```python
import functools
import math

import jax
import jax.numpy as jnp
from jax import lax
from jax.experimental import pallas as pl
from jax.experimental.pallas import tpu as pltpu
from jax.sharding import PartitionSpec as P

MESH = pl.DeviceIdType.MESH
F32 = jnp.float32
BF16 = jnp.bfloat16
WIRE = jnp.int16
TOP = 32000.0
VMEM_LIMIT = 56 * 1024 * 1024

NN = (((1,), (0,)), ((), ()))
NT = (((1,), (1,)), ((), ()))
TN = (((0,), (0,)), ((), ()))


def mm(a, b, dims):
    return lax.dot_general(a, b, dims, preferred_element_type=F32)


def split(x):
    hi = x.astype(BF16)
    return hi, (x - hi.astype(F32)).astype(BF16)


def encode(x, scale):
    v = jnp.abs(x) * scale
    u = v * lax.rsqrt(v + 1e-30)
    return jnp.round(jnp.where(x < 0, -u, u)).astype(jnp.int32).astype(WIRE)


def decode(code, unit):
    u = code.astype(jnp.int32).astype(F32)
    return u * jnp.abs(u) * unit


def slot_table(coords, count):
    slots = coords.shape[1]
    sub = lax.broadcasted_iota(jnp.int32, (slots, slots), 0)
    lane = lax.broadcasted_iota(jnp.int32, (slots, slots), 1)
    dead = 1 << 12
    key = jnp.where(lane < count, jnp.broadcast_to(coords, (slots, slots)), dead)
    flip = jnp.sum(jnp.where(sub == lane, key, 0), axis=1, keepdims=True)
    same = (key == flip) & (lane < sub)
    ahead = jnp.sum(jnp.where((key < flip) | same, 1, 0), axis=1, keepdims=True)
    keep = jnp.minimum(jnp.sum(jnp.where(same, 1, 0), axis=1, keepdims=True), 1)
    place = lax.broadcasted_iota(jnp.int32, (slots, 128), 1)
    slot = lax.broadcasted_iota(jnp.int32, (slots, 128), 0)
    match = ahead == place

    def down(x):
        return jnp.sum(x, axis=0, keepdims=True)

    order = down(jnp.where(match, slot, 0))
    goes_on = down(jnp.where(match, keep, 0))
    last = jnp.maximum(down(jnp.where(flip <= place, 1, 0)) - 1, 0)
    named = jnp.minimum(down(jnp.where(flip == place, 1, 0)), 1)
    return [order, goes_on, last, named]


def layer_kernel(
    rz, rp, cn, norm,
    order, feat, weight, bias, grad_hidden, coords, counts, tiles,
    hid_out, gf_out, gw_out, gb_out,
    buf, run, table, places, ahi, alo, xall, yfull, wall, hall, gp, kept, c1send, c1recv, c2send, c2recv,
    g1send, g1recv, g2send, g2recv, gall, s1send, s1recv, s2send, s2recv,
    a_sem, x_ss, x_rs, y_ss, y_rs, w_ss, w_rs, h_ss, h_rs, c1_ss, c1_rs, c2_ss, c2_rs,
    g1_ss, g1_rs, g2_ss, g2_rs, g3_ss, g3_rs, s1_ss, s1_rs, s2_ss, s2_rs,
):
    row, col = lax.axis_index("row"), lax.axis_index("col")
    zi, pi = row // rp, lax.rem(row, rp)
    fl, nodes = feat.shape
    hl = weight.shape[1]
    fin = weight.shape[0]
    fr = fin // rp

    def zmate(d):
        return (lax.rem(zi + d, rz) * rp + pi, col)

    def pmate(d):
        return (zi * rp + lax.rem(pi + d, rp), col)

    def cmate(d):
        return (row, lax.rem(col + d, cn))

    mates = [zmate(d) for d in range(1, rz)]
    mates += [pmate(d) for d in range(1, rp)]
    mates += [cmate(d) for d in range(1, cn)]

    def remote(src, dst, ss, rs, to):
        return pltpu.make_async_remote_copy(
            src_ref=src, dst_ref=dst, send_sem=ss, recv_sem=rs,
            device_id=to, device_id_type=MESH,
        )

    rows, slots, tile, _ = buf.shape
    loads = [pltpu.make_async_copy(tiles.at[i], buf.at[i], a_sem.at[i]) for i in range(rows)]
    for c in loads:
        c.start()
    barrier = pltpu.get_barrier_semaphore()
    for mate in mates:
        pl.semaphore_signal(barrier, inc=1, device_id=mate, device_id_type=MESH)

    lines = []
    for i in range(rows):
        lines += slot_table(coords[i:i + 1, :], counts[i])
    table[...] = jnp.concatenate(lines, axis=0)
    to_places = pltpu.make_async_copy(table, places, a_sem.at[rows])
    to_places.start()

    local = order[...] - row * nodes
    pick = (lax.broadcasted_iota(jnp.int32, (nodes, nodes), 0) == local).astype(F32).astype(BF16)
    xall[0, 0] = mm(feat[...], pick, NN).astype(BF16)
    first = lax.broadcasted_iota(jnp.int32, (16, hl), 0) == 0
    wall[0, :fin, :] = weight[...]
    hall[0] = grad_hidden[...]
    wall[0, fin:, :] = jnp.where(first, bias[...].astype(F32), 0.0).astype(BF16)
    pl.semaphore_wait(barrier, len(mates))

    sent = []

    def go(c):
        c.start()
        sent.append(c)
        return c

    def each(low, high, body, unroll=1):
        def run_body(n, carry):
            body(n)
            return carry

        lax.fori_loop(low, high, run_body, 0, unroll=unroll)

    def xz(d):
        return remote(xall.at[0, 0], xall.at[d, 0], x_ss.at[d, 0], x_rs.at[d, 0], zmate(d))

    def xp(dz, dp):
        return remote(xall.at[dz, 0], xall.at[dz, dp], x_ss.at[dz, dp], x_rs.at[dz, dp],
                      pmate(dp))

    def relay(dz):
        each(1, rp, lambda dp: xp(dz, dp).start())

    each(1, rz, lambda d: xz(d).start())
    relay(0)
    wx = [go(remote(wall.at[0], wall.at[d], w_ss.at[d], w_rs.at[d], cmate(d)))
          for d in range(1, cn)]
    hx = [go(remote(hall.at[0], hall.at[d], h_ss.at[d], h_rs.at[d], cmate(d)))
          for d in range(1, cn)]
    to_places.wait()
    for c in loads:
        c.wait()

    def add(s, sums):
        new = []
        for i in range(rows):
            keep = places[4 * i + 1, s].astype(F32)
            total = sums[i] * keep + buf[i, jnp.clip(places[4 * i, s], 0, slots - 1)].astype(F32)
            run[i, s] = total
            new.append(total)
        return tuple(new)

    sums = tuple(jnp.zeros((tile, tile), F32) for _ in range(rows))
    step = slots // rz

    def segment(n, sums):
        sums = lax.fori_loop(0, step, lambda k, c: add((n - 1) * step + k, c), sums, unroll=2)
        xz(n).wait_recv()
        relay(n)
        return sums

    sums = lax.fori_loop(1, rz, segment, sums)
    lax.fori_loop((rz - 1) * step, slots, add, sums, unroll=2)

    def place(p, top):
        for h in range(rows):
            squares = jnp.zeros((1, tile), F32)
            for i in range(rows):
                j = p * rows + h
                named = places[4 * i + 3, j].astype(F32)
                dense = run[i, jnp.clip(places[4 * i + 2, j], 0, slots - 1)] * named
                hi, lo = split(dense)
                ahi[p, i * tile:(i + 1) * tile, h * tile:(h + 1) * tile] = hi
                alo[p, i * tile:(i + 1) * tile, h * tile:(h + 1) * tile] = lo
                squares = squares + jnp.sum(dense * dense, axis=0, keepdims=True)
            top = jnp.maximum(top, squares)
        return top

    def piece(dz, dp):
        return lax.rem(zi + rz - dz, rz) * rp + lax.rem(pi + rp - dp, rp)

    top = lax.fori_loop(0, rz * rp, place, jnp.zeros((1, tile), F32))

    def terms(dz, y):
        each(1, rp, lambda dp: xp(dz, dp).wait_recv())
        for dp in range(rp):
            at = piece(dz, dp)
            x = xall[dz, dp]
            y = y + mm(x, ahi[at], NT) + mm(x, alo[at], NT)
        return y

    y = lax.fori_loop(0, rz, terms, jnp.zeros((fl, nodes), F32))

    mine = pl.ds(pl.multiple_of(col * fl, fl), fl)
    yfull[mine, :] = y
    yx = [go(remote(yfull.at[mine], yfull.at[mine], y_ss.at[d], y_rs.at[d], cmate(d)))
          for d in range(1, cn)]
    for c in yx:
        c.wait_recv()
    for c in wx + hx:
        c.wait_recv()
    y_hi, y_lo = split(yfull[...])
    ones = jnp.ones((16, nodes), BF16)
    y_ext = jnp.concatenate([y_hi, ones], axis=0)

    def units(n, z):
        d = cn - 1 - n
        pre = mm(wall[d], y_ext, TN) + mm(wall[d, :fin, :], y_lo, TN)
        gate = jax.nn.sigmoid(pre)
        grad_pre = hall[d].astype(F32) * gate * (1.0 + pre * (1.0 - gate))
        part_hi, part_lo = split(grad_pre)
        hid_out[...] = (pre * gate).astype(BF16)
        gp[0] = part_hi
        gp[1] = part_lo
        here = wall[d, mine, :]
        return z + mm(here, part_hi, NN) + mm(here, part_lo, NN)

    z = lax.fori_loop(0, cn, units, jnp.zeros((fl, nodes), F32))

    longest = jnp.max(jnp.sum(z * z, axis=1, keepdims=True), axis=0, keepdims=True)
    bound = jnp.sqrt(longest * jnp.max(top, keepdims=True)) + 1e-16
    s1send[...] = jnp.broadcast_to(bound, s1send.shape)
    s1 = [go(remote(s1send, s1recv.at[d], s1_ss.at[d], s1_rs.at[d], pmate(d)))
          for d in range(1, rp)]
    up = TOP * TOP / bound
    z_hi, z_lo = split(z)
    z_two = jnp.concatenate([z_hi, z_lo], axis=0)

    def c1(d, dp):
        return remote(c1send.at[d, dp], c1recv.at[d, dp], c1_ss.at[d, dp], c1_rs.at[d, dp],
                      pmate(dp))

    def c2(d):
        return remote(c2send.at[d], c2recv.at[d], c2_ss.at[d], c2_rs.at[d], zmate(d))

    def contribute(d):
        for dp in list(range(1, rp)) + [0]:
            at = lax.rem(zi + d, rz) * rp + lax.rem(pi + dp, rp)
            both = mm(z_two, ahi[at], NN)
            c = both[:fl] + both[fl:] + mm(z_hi, alo[at], NN)
            if dp == 0:
                kept[d] = c
            else:
                c1send[d, dp] = encode(c, up)
                c1(d, dp).start()

    def reduced(d):
        total = kept[d]
        for dp in range(1, rp):
            c1(d, dp).wait_recv()
            total = total + decode(c1recv[d, dp], s1recv[dp, :1, :1] * (1.0 / TOP / TOP))
        return total

    contribute(1)

    gw = mm(y_ext, gp[0], NT) + mm(y_ext, gp[1], NT)
    gb = gw[fin:fin + 8]
    gw = gw[:fin] + mm(y_lo, gp[0], NT)
    for q in range(rp):
        g1send[q, :fr] = gw[q * fr:(q + 1) * fr]
        g1send[q, fr:] = gb
    g1 = [go(remote(g1send.at[lax.rem(pi + d, rp)], g1recv.at[d], g1_ss.at[d], g1_rs.at[d],
                    pmate(d))) for d in range(1, rp)]

    for d in range(1, rp):
        s1[d - 1].wait_recv()
        bound = bound + s1recv[d, :1, :1]
    s2send[...] = jnp.broadcast_to(bound, s2send.shape)
    s2 = [go(remote(s2send, s2recv.at[d], s2_ss.at[d], s2_rs.at[d], zmate(d)))
          for d in range(1, rz)]
    up2 = TOP * TOP / bound

    part = g1send[pi]
    for d in range(1, rp):
        g1[d - 1].wait_recv()
        part = part + g1recv[d]
    g2send[...] = part
    g2 = [go(remote(g2send, g2recv.at[d], g2_ss.at[d], g2_rs.at[d], zmate(d)))
          for d in range(1, rz)]

    def onward(d):
        contribute(lax.rem(d + 1, rz))
        c2send[d] = encode(reduced(d), up2)
        c2(d).start()

    each(1, rz, onward)
    for d in range(1, rz):
        g2[d - 1].wait_recv()
        part = part + g2recv[d]
    gall[pi] = part[:fr]
    g3 = [go(remote(gall.at[pi], gall.at[pi], g3_ss.at[d], g3_rs.at[d], pmate(d)))
          for d in range(1, rp)]
    gb_out[...] = part[fr:fr + 1] * norm
    total = reduced(0)
    for c in g3:
        c.wait_recv()
    gw_out[...] = gall[...].reshape(fin, hl) * norm
    for d in range(1, rz):
        s2[d - 1].wait_recv()
        c2(d).wait_recv()
        total = total + decode(c2recv[d], s2recv[d, :1, :1] * (1.0 / TOP / TOP))
    gf_out[...] = total
    for c in sent:
        c.wait_send()

    def all_sent(d):
        each(1, rp, lambda dp: xp(d, dp).wait_send())
        each(1, rp, lambda dp: c1(d, dp).wait_send())

    def all_passed(d):
        xz(d).wait_send()
        c2(d).wait_send()

    each(0, rz, all_sent)
    each(1, rz, all_passed)


def hand_over(*refs):
    half = len(refs) // 2
    for source, target in zip(refs[:half], refs[half:]):
        target[...] = source[...]


def per_device(r, cn, features, order, weight, bias, tiles, coords, counts, grad_hidden):
    rows, slots, tile, _ = tiles.shape
    nodes = order.shape[0]
    fl = features.shape[0]
    fin, hl = weight.shape
    rz = 4
    assert r % rz == 0 and slots % 4 == 0 and r * rows <= 128
    rp = r // rz
    fr = fin // rp
    norm = 1.0 / math.sqrt(nodes * r)
    vmem = pl.BlockSpec(memory_space=pltpu.VMEM)
    smem = pl.BlockSpec(memory_space=pltpu.SMEM)
    anyw = pl.BlockSpec(memory_space=pl.ANY)
    dma = pltpu.SemaphoreType.DMA
    outs = (
        jax.ShapeDtypeStruct((hl, nodes), BF16),
        jax.ShapeDtypeStruct((fl, nodes), F32),
        jax.ShapeDtypeStruct((fin, hl), F32),
        jax.ShapeDtypeStruct((1, hl), F32),
    )
    hidden, gf, gw, gb = pl.pallas_call(
        functools.partial(layer_kernel, rz, rp, cn, norm),
        out_shape=outs,
        in_specs=[vmem] * 6 + [smem, anyw],
        out_specs=(vmem,) * 4,
        scratch_shapes=[
            pltpu.VMEM((rows, slots, tile, tile), BF16),
            pltpu.VMEM((rows, slots, tile, tile), F32),
            pltpu.VMEM((4 * rows, 128), jnp.int32),
            pltpu.SMEM((4 * rows, 128), jnp.int32),
            pltpu.VMEM((r, nodes, nodes), BF16),
            pltpu.VMEM((r, nodes, nodes), BF16),
            pltpu.VMEM((rz, rp, fl, nodes), BF16),
            pltpu.VMEM((fin, nodes), F32),
            pltpu.VMEM((cn, fin + 16, hl), BF16),
            pltpu.VMEM((cn, hl, nodes), BF16),
            pltpu.VMEM((2, hl, nodes), BF16),
            pltpu.VMEM((rz, fl, nodes), F32),
            pltpu.VMEM((rz, rp, fl, nodes), WIRE),
            pltpu.VMEM((rz, rp, fl, nodes), WIRE),
            pltpu.VMEM((rz, fl, nodes), WIRE),
            pltpu.VMEM((rz, fl, nodes), WIRE),
            pltpu.VMEM((rp, fr + 8, hl), F32),
            pltpu.VMEM((rp, fr + 8, hl), F32),
            pltpu.VMEM((fr + 8, hl), F32),
            pltpu.VMEM((rz, fr + 8, hl), F32),
            pltpu.VMEM((rp, fr, hl), F32),
            pltpu.VMEM((8, 128), F32),
            pltpu.VMEM((rp, 8, 128), F32),
            pltpu.VMEM((8, 128), F32),
            pltpu.VMEM((rz, 8, 128), F32),
            dma((rows + 1,)),
            dma((rz, rp)), dma((rz, rp)),
            dma((cn,)), dma((cn,)),
            dma((cn,)), dma((cn,)),
            dma((cn,)), dma((cn,)),
            dma((rz, rp)), dma((rz, rp)),
            dma((rz,)), dma((rz,)),
            dma((rp,)), dma((rp,)),
            dma((rz,)), dma((rz,)),
            dma((rp,)), dma((rp,)),
            dma((rp,)), dma((rp,)),
            dma((rz,)), dma((rz,)),
        ],
        compiler_params=pltpu.CompilerParams(
            collective_id=0, has_side_effects=True, vmem_limit_bytes=VMEM_LIMIT
        ),
        name="layer",
    )(order.reshape(1, nodes), features, weight, bias.reshape(1, hl), grad_hidden, coords, counts, tiles)
    hidden, gf, gw, gb = pl.pallas_call(
        hand_over,
        out_shape=outs,
        in_specs=[vmem] * 4,
        out_specs=(vmem,) * 4,
        name="hand_over",
    )(hidden, gf, gw, gb)
    return hidden, gf, gw, gb.reshape(hl)


def solution(mesh):
    in_specs = (
        P("col", "row"),
        P("row"),
        P(None, "col"),
        P("col"),
        P("row", None, None, None),
        P("row", None),
        P("row"),
        P("col", "row"),
    )
    out_specs = (P("col", "row"), P("col", "row"), P(None, "col"), P("col"))
    return jax.shard_map(
        functools.partial(per_device, mesh.shape["row"], mesh.shape["col"]),
        mesh=mesh, in_specs=in_specs, out_specs=out_specs, check_vma=False,
    )
```

```python
import functools
import math

import jax
import jax.numpy as jnp
from jax import lax
from jax.experimental import pallas as pl
from jax.experimental.pallas import tpu as pltpu
from jax.sharding import PartitionSpec as P

MESH = pl.DeviceIdType.MESH
F32 = jnp.float32
BF16 = jnp.bfloat16
WIRE = jnp.int16
TOP = 32000.0
VMEM_LIMIT = 56 * 1024 * 1024

NN = (((1,), (0,)), ((), ()))
NT = (((1,), (1,)), ((), ()))
TN = (((0,), (0,)), ((), ()))


def mm(a, b, dims):
    return lax.dot_general(a, b, dims, preferred_element_type=F32)


def split(x):
    hi = x.astype(BF16)
    return hi, (x - hi.astype(F32)).astype(BF16)


def encode(x, scale):
    v = jnp.abs(x) * scale
    u = v * lax.rsqrt(v + 1e-30)
    return jnp.round(jnp.where(x < 0, -u, u)).astype(jnp.int32).astype(WIRE)


def decode(code, unit):
    u = code.astype(jnp.int32).astype(F32)
    return u * jnp.abs(u) * unit


def slot_table(coords, count):
    slots = coords.shape[1]
    sub = lax.broadcasted_iota(jnp.int32, (slots, slots), 0)
    lane = lax.broadcasted_iota(jnp.int32, (slots, slots), 1)
    dead = 1 << 12
    key = jnp.where(lane < count, jnp.broadcast_to(coords, (slots, slots)), dead)
    flip = jnp.sum(jnp.where(sub == lane, key, 0), axis=1, keepdims=True)
    same = (key == flip) & (lane < sub)
    ahead = jnp.sum(jnp.where((key < flip) | same, 1, 0), axis=1, keepdims=True)
    keep = jnp.minimum(jnp.sum(jnp.where(same, 1, 0), axis=1, keepdims=True), 1)
    place = lax.broadcasted_iota(jnp.int32, (slots, 128), 1)
    slot = lax.broadcasted_iota(jnp.int32, (slots, 128), 0)
    match = ahead == place

    def down(x):
        return jnp.sum(x, axis=0, keepdims=True)

    order = down(jnp.where(match, slot, 0))
    goes_on = down(jnp.where(match, keep, 0))
    last = jnp.maximum(down(jnp.where(flip <= place, 1, 0)) - 1, 0)
    named = jnp.minimum(down(jnp.where(flip == place, 1, 0)), 1)
    return [order, goes_on, last, named]


def layer_kernel(
    rz, rp, cn, norm,
    order, feat, weight, bias, grad_hidden, coords, counts, tiles,
    hid_out, gf_out, gw_out, gb_out,
    buf, run, table, places, ahi, alo, xall, yfull, zpart, zrecv, c1send, c1recv, c2send, c2recv,
    g1send, g1recv, g2send, g2recv, gall, s1send, s1recv, s2send, s2recv,
    a_sem, x_ss, x_rs, y_ss, y_rs, z_ss, z_rs, c1_ss, c1_rs, c2_ss, c2_rs,
    g1_ss, g1_rs, g2_ss, g2_rs, g3_ss, g3_rs, s1_ss, s1_rs, s2_ss, s2_rs,
):
    row, col = lax.axis_index("row"), lax.axis_index("col")
    zi, pi = row // rp, lax.rem(row, rp)
    fl, nodes = feat.shape
    hl = weight.shape[1]
    fin = weight.shape[0]
    fr = fin // rp

    def zmate(d):
        return (lax.rem(zi + d, rz) * rp + pi, col)

    def pmate(d):
        return (zi * rp + lax.rem(pi + d, rp), col)

    def cmate(d):
        return (row, lax.rem(col + d, cn))

    mates = [zmate(d) for d in range(1, rz)]
    mates += [pmate(d) for d in range(1, rp)]
    mates += [cmate(d) for d in range(1, cn)]

    def remote(src, dst, ss, rs, to):
        return pltpu.make_async_remote_copy(
            src_ref=src, dst_ref=dst, send_sem=ss, recv_sem=rs,
            device_id=to, device_id_type=MESH,
        )

    rows, slots, tile, _ = buf.shape
    loads = [pltpu.make_async_copy(tiles.at[i], buf.at[i], a_sem.at[i]) for i in range(rows)]
    for c in loads:
        c.start()
    barrier = pltpu.get_barrier_semaphore()
    for mate in mates:
        pl.semaphore_signal(barrier, inc=1, device_id=mate, device_id_type=MESH)

    lines = []
    for i in range(rows):
        lines += slot_table(coords[i:i + 1, :], counts[i])
    table[...] = jnp.concatenate(lines, axis=0)
    to_places = pltpu.make_async_copy(table, places, a_sem.at[rows])
    to_places.start()

    local = order[...] - row * nodes
    pick = (lax.broadcasted_iota(jnp.int32, (nodes, nodes), 0) == local).astype(F32).astype(BF16)
    xall[0, 0] = mm(feat[...], pick, NN).astype(BF16)
    pl.semaphore_wait(barrier, len(mates))

    sent = []

    def go(c):
        c.start()
        sent.append(c)
        return c

    xz = {d: go(remote(xall.at[0, 0], xall.at[d, 0], x_ss.at[d, 0], x_rs.at[d, 0], zmate(d)))
          for d in range(1, rz)}
    xp = {}

    def relay(dz):
        for dp in range(1, rp):
            xp[dz, dp] = go(remote(xall.at[dz, 0], xall.at[dz, dp], x_ss.at[dz, dp],
                                   x_rs.at[dz, dp], pmate(dp)))

    relay(0)
    to_places.wait()
    for c in loads:
        c.wait()

    def add(s, sums):
        new = []
        for i in range(rows):
            keep = places[4 * i + 1, s].astype(F32)
            total = sums[i] * keep + buf[i, jnp.clip(places[4 * i, s], 0, slots - 1)].astype(F32)
            run[i, s] = total
            new.append(total)
        return tuple(new)

    sums = tuple(jnp.zeros((tile, tile), F32) for _ in range(rows))
    near = [1, 3, 2]
    step = slots // 4
    for n in range(4):
        sums = lax.fori_loop(n * step, (n + 1) * step, add, sums)
        if n < 3:
            xz[near[n]].wait_recv()
            relay(near[n])

    def place(p, top):
        for h in range(rows):
            squares = jnp.zeros((1, tile), F32)
            for i in range(rows):
                j = p * rows + h
                named = places[4 * i + 3, j].astype(F32)
                dense = run[i, jnp.clip(places[4 * i + 2, j], 0, slots - 1)] * named
                hi, lo = split(dense)
                ahi[p, i * tile:(i + 1) * tile, h * tile:(h + 1) * tile] = hi
                alo[p, i * tile:(i + 1) * tile, h * tile:(h + 1) * tile] = lo
                squares = squares + jnp.sum(dense * dense, axis=0, keepdims=True)
            top = jnp.maximum(top, squares)
        return top

    top = lax.fori_loop(0, rz * rp, place, jnp.zeros((1, tile), F32))

    def piece(dz, dp):
        return lax.rem(zi + rz - dz, rz) * rp + lax.rem(pi + rp - dp, rp)

    def term(dz, dp):
        at = piece(dz, dp)
        x = xall[dz, dp]
        return mm(x, ahi[at], NT) + mm(x, alo[at], NT)

    y = term(0, 0)
    for dz in near:
        y = y + term(dz, 0)
    for dz in [0] + near:
        for dp in range(1, rp):
            xp[dz, dp].wait_recv()
        for dp in range(1, rp):
            y = y + term(dz, dp)

    mine = pl.ds(pl.multiple_of(col * fl, fl), fl)
    yfull[mine, :] = y
    yx = [go(remote(yfull.at[mine], yfull.at[mine], y_ss.at[d], y_rs.at[d], cmate(d)))
          for d in range(1, cn)]
    for c in yx:
        c.wait_recv()
    y_hi, y_lo = split(yfull[...])

    w = weight[...]
    first = lax.broadcasted_iota(jnp.int32, (16, hl), 0) == 0
    bias_rows = jnp.where(first, bias[...].astype(F32), 0.0).astype(BF16)
    pre = mm(w, y_hi, TN) + mm(w, y_lo, TN) + mm(bias_rows, jnp.ones((16, nodes), BF16), TN)
    gate = jax.nn.sigmoid(pre)
    hid_out[...] = (pre * gate).astype(BF16)
    grad_pre = grad_hidden[...].astype(F32) * gate * (1.0 + pre * (1.0 - gate))
    gp_hi, gp_lo = split(grad_pre)

    zpart[...] = mm(w, gp_hi, NN) + mm(w, gp_lo, NN)
    zx = []
    for d in range(1, cn):
        theirs = pl.ds(pl.multiple_of(lax.rem(col + d, cn) * fl, fl), fl)
        zx.append(go(remote(zpart.at[theirs], zrecv.at[d], z_ss.at[d], z_rs.at[d], cmate(d))))

    gw = mm(y_hi, gp_hi, NT) + mm(y_lo, gp_hi, NT) + mm(y_hi, gp_lo, NT)
    ones = jnp.ones((16, nodes), BF16)
    gb = (mm(ones, gp_hi, NT) + mm(ones, gp_lo, NT))[:8]
    for q in range(rp):
        g1send[q, :fr] = gw[q * fr:(q + 1) * fr]
        g1send[q, fr:] = gb
    g1 = [go(remote(g1send.at[lax.rem(pi + d, rp)], g1recv.at[d], g1_ss.at[d], g1_rs.at[d],
                    pmate(d))) for d in range(1, rp)]

    z = zpart[mine, :]
    for d in range(1, cn):
        zx[d - 1].wait_recv()
        z = z + zrecv[d]
    longest = jnp.max(jnp.sum(z * z, axis=1, keepdims=True), axis=0, keepdims=True)
    bound = jnp.sqrt(longest * jnp.max(top, keepdims=True)) + 1e-16
    s1send[...] = jnp.broadcast_to(bound, s1send.shape)
    s1 = [go(remote(s1send, s1recv.at[d], s1_ss.at[d], s1_rs.at[d], pmate(d)))
          for d in range(1, rp)]
    up = TOP * TOP / bound
    z_hi, z_lo = split(z)
    z_two = jnp.concatenate([z_hi, z_lo], axis=0)

    c1 = {}
    kept = {}

    def contribute(d):
        parts = []
        for dp in range(rp):
            at = lax.rem(zi + d, rz) * rp + lax.rem(pi + dp, rp)
            both = mm(z_two, ahi[at], NN)
            parts.append(both[:fl] + both[fl:] + mm(z_hi, alo[at], NN))
        kept[d] = parts[0]
        for dp in range(1, rp):
            c1send[d, dp] = encode(parts[dp], up)
        for dp in range(1, rp):
            c1[d, dp] = go(remote(c1send.at[d, dp], c1recv.at[d, dp], c1_ss.at[d, dp],
                                  c1_rs.at[d, dp], pmate(dp)))

    def reduced(d):
        total = kept[d]
        for dp in range(1, rp):
            c1[d, dp].wait_recv()
        for dp in range(1, rp):
            total = total + decode(c1recv[d, dp], down[dp])
        return total

    c2 = {}

    def pass_on(d):
        c2send[d] = encode(reduced(d), up2)
        c2[d] = go(remote(c2send.at[d], c2recv.at[d], c2_ss.at[d], c2_rs.at[d], zmate(d)))

    contribute(1)
    contribute(2)

    part = g1send[pi]
    for d in range(1, rp):
        g1[d - 1].wait_recv()
        part = part + g1recv[d]
    g2send[...] = part
    g2 = [go(remote(g2send, g2recv.at[d], g2_ss.at[d], g2_rs.at[d], zmate(d)))
          for d in range(1, rz)]
    down = {}
    for d in range(1, rp):
        s1[d - 1].wait_recv()
        down[d] = s1recv[d, :1, :1] * (1.0 / TOP / TOP)
        bound = bound + s1recv[d, :1, :1]
    s2send[...] = jnp.broadcast_to(bound, s2send.shape)
    s2 = [go(remote(s2send, s2recv.at[d], s2_ss.at[d], s2_rs.at[d], zmate(d)))
          for d in range(1, rz)]
    up2 = TOP * TOP / bound

    pass_on(1)
    for d in range(3, rz):
        contribute(d)
        pass_on(d - 1)
    contribute(0)
    for d in range(1, rz):
        g2[d - 1].wait_recv()
        part = part + g2recv[d]
    gall[pi] = part[:fr]
    g3 = [go(remote(gall.at[pi], gall.at[pi], g3_ss.at[d], g3_rs.at[d], pmate(d)))
          for d in range(1, rp)]
    gb_out[...] = part[fr:fr + 1] * norm
    pass_on(rz - 1)
    total = reduced(0)
    for c in g3:
        c.wait_recv()
    gw_out[...] = gall[...].reshape(fin, hl) * norm
    for d in range(1, rz):
        s2[d - 1].wait_recv()
        c2[d].wait_recv()
        total = total + decode(c2recv[d], s2recv[d, :1, :1] * (1.0 / TOP / TOP))
    gf_out[...] = total
    for c in sent:
        c.wait_send()


def hand_over(*refs):
    half = len(refs) // 2
    for source, target in zip(refs[:half], refs[half:]):
        target[...] = source[...]


def per_device(r, cn, features, order, weight, bias, tiles, coords, counts, grad_hidden):
    rows, slots, tile, _ = tiles.shape
    nodes = order.shape[0]
    fl = features.shape[0]
    fin, hl = weight.shape
    rz = 4
    assert r % rz == 0 and slots % 4 == 0 and r * rows <= 128
    rp = r // rz
    fr = fin // rp
    norm = 1.0 / math.sqrt(nodes * r)
    vmem = pl.BlockSpec(memory_space=pltpu.VMEM)
    smem = pl.BlockSpec(memory_space=pltpu.SMEM)
    anyw = pl.BlockSpec(memory_space=pl.ANY)
    dma = pltpu.SemaphoreType.DMA
    outs = (
        jax.ShapeDtypeStruct((hl, nodes), BF16),
        jax.ShapeDtypeStruct((fl, nodes), F32),
        jax.ShapeDtypeStruct((fin, hl), F32),
        jax.ShapeDtypeStruct((1, hl), F32),
    )
    hidden, gf, gw, gb = pl.pallas_call(
        functools.partial(layer_kernel, rz, rp, cn, norm),
        out_shape=outs,
        in_specs=[vmem] * 6 + [smem, anyw],
        out_specs=(vmem,) * 4,
        scratch_shapes=[
            pltpu.VMEM((rows, slots, tile, tile), BF16),
            pltpu.VMEM((rows, slots, tile, tile), F32),
            pltpu.VMEM((4 * rows, 128), jnp.int32),
            pltpu.SMEM((4 * rows, 128), jnp.int32),
            pltpu.VMEM((r, nodes, nodes), BF16),
            pltpu.VMEM((r, nodes, nodes), BF16),
            pltpu.VMEM((rz, rp, fl, nodes), BF16),
            pltpu.VMEM((fin, nodes), F32),
            pltpu.VMEM((fin, nodes), F32),
            pltpu.VMEM((cn, fl, nodes), F32),
            pltpu.VMEM((rz, rp, fl, nodes), WIRE),
            pltpu.VMEM((rz, rp, fl, nodes), WIRE),
            pltpu.VMEM((rz, fl, nodes), WIRE),
            pltpu.VMEM((rz, fl, nodes), WIRE),
            pltpu.VMEM((rp, fr + 8, hl), F32),
            pltpu.VMEM((rp, fr + 8, hl), F32),
            pltpu.VMEM((fr + 8, hl), F32),
            pltpu.VMEM((rz, fr + 8, hl), F32),
            pltpu.VMEM((rp, fr, hl), F32),
            pltpu.VMEM((8, 128), F32),
            pltpu.VMEM((rp, 8, 128), F32),
            pltpu.VMEM((8, 128), F32),
            pltpu.VMEM((rz, 8, 128), F32),
            dma((rows + 1,)),
            dma((rz, rp)), dma((rz, rp)),
            dma((cn,)), dma((cn,)),
            dma((cn,)), dma((cn,)),
            dma((rz, rp)), dma((rz, rp)),
            dma((rz,)), dma((rz,)),
            dma((rp,)), dma((rp,)),
            dma((rz,)), dma((rz,)),
            dma((rp,)), dma((rp,)),
            dma((rp,)), dma((rp,)),
            dma((rz,)), dma((rz,)),
        ],
        compiler_params=pltpu.CompilerParams(
            collective_id=0, has_side_effects=True, vmem_limit_bytes=VMEM_LIMIT
        ),
        name="layer",
    )(order.reshape(1, nodes), features, weight, bias.reshape(1, hl), grad_hidden, coords, counts, tiles)
    hidden, gf, gw, gb = pl.pallas_call(
        hand_over,
        out_shape=outs,
        in_specs=[vmem] * 4,
        out_specs=(vmem,) * 4,
        name="hand_over",
    )(hidden, gf, gw, gb)
    return hidden, gf, gw, gb.reshape(hl)


def solution(mesh):
    in_specs = (
        P("col", "row"),
        P("row"),
        P(None, "col"),
        P("col"),
        P("row", None, None, None),
        P("row", None),
        P("row"),
        P("col", "row"),
    )
    out_specs = (P("col", "row"), P("col", "row"), P(None, "col"), P("col"))
    return jax.shard_map(
        functools.partial(per_device, mesh.shape["row"], mesh.shape["col"]),
        mesh=mesh, in_specs=in_specs, out_specs=out_specs, check_vma=False,
    )
```
